256 devices in a mesh: dp: 16 (over y_hi, z), mp: 16 (over x, y_lo, core).
Axes of the slice: x: 4, y: 4 (y_hi: 2, y_lo: 2; y = y_hi * 2 + y_lo), z: 8, core: 2. Of those that a mesh axis runs over, the one named last changes fastest.
Arguments:
- tokens: bfloat16 [2048, 8192], P('dp', 'mp'), may hold values from -6 to 6
- pattern: int32 [128, 16], P('mp'), may hold values from 0 to 63, all different within a row
- w_up: bfloat16 [128, 16, 128, 128], P('mp', 'dp'), may hold values from -0.125 to 0.125
- w_down: bfloat16 [128, 16, 128, 128], P('mp', 'dp'), may hold values from -0.09375 to 0.09375
- cotangent: bfloat16 [2048, 8192], P('dp', 'mp'), may hold values from -6 to 6
Outputs:
- mixed: bfloat16 [2048, 8192], P('dp', 'mp')
- grad_tokens: bfloat16 [2048, 8192], P('dp', 'mp')
- grad_up: float32 [128, 16, 128, 128], P('mp', 'dp')
- grad_down: float32 [128, 16, 128, 128], P('mp', 'dp')
The draws below stay inside these ranges and needn't reach their ends.
Inputs may be any that keep to these rules, and one draw needn't show every extreme that they name: Each row of pattern names 16 different block rows; every block row is named by some row.
All inputs are finite; a program needn't handle non-finite values.
Results may differ from the reference program's by a relative error of at most 0.02.
Values may be sent and summed in bfloat16 or wider, within the bound.
No kernel may reach another device: no remote copies, remote signals or barrier semaphores. Data moves between devices by JAX's collectives and lax.ppermute only.
A program may use at most 128 MiB of HBM per device.

```python
import jax
import jax.numpy as jnp
from jax import lax

D = 8192
FF = 16384
BLK = 128
TOK_DEV = 128
NBD = 64
NBF = 128
KEEP = 16
TOKENS = 2048
N_DP = 16
N_MP = 16


def steps_of(own_key, dims, cuts, smallest, largest):
    gain = 1.0
    for axis_at, shards_of in cuts:
        heights = jax.random.uniform(jax.random.fold_in(jax.random.fold_in(own_key, 6), axis_at), (shards_of,), jnp.float32, smallest / len(cuts), largest / len(cuts))
        gain = gain * jnp.repeat(jnp.exp(heights), dims[axis_at] // shards_of).reshape((-1,) + (1,) * (len(dims) - 1 - axis_at))
    return gain


def choose_distinct(rng, rows, number_of, top, lift):
    sequence = jax.random.permutation(jax.random.fold_in(rng, 1), number_of)
    boost = sequence
    for power in range(3):
        boost = boost * boost // number_of
    boost = boost * lift // number_of
    chance = jax.random.randint(jax.random.fold_in(rng, 2), (rows, number_of), 0, 4096) + boost
    holders = jax.random.permutation(jax.random.fold_in(rng, 3), rows)[jnp.arange(number_of) % rows]
    chance = jnp.where(jnp.arange(rows)[:, None] == holders[None, :], 1 << 14, chance)
    priority = chance * number_of + jnp.arange(number_of)
    return lax.top_k(priority.astype(jnp.int32), top)[1].astype(jnp.int32)


def gaussian(key, dims, scale, reach, pieces=(), held_as=jnp.bfloat16):
    drawn = jax.random.normal(key, dims, jnp.float32) * scale
    if len(pieces) > 0:
        drawn = steps_of(key, dims, pieces, -0.22, 0.18) * drawn
    return jnp.clip(drawn, min=-reach, max=reach).astype(held_as)


def setup_inputs(seed: int = 0) -> dict:
    seeds = jax.random.split(jax.random.key(seed), 6)
    tokens = gaussian(seeds[0], (TOKENS, D), 1.0, 6.0, ((0, 16), (1, 16)))
    pattern = choose_distinct(seeds[1], NBF, NBD, KEEP, 4096)
    w_up = gaussian(seeds[2], (NBF, KEEP, BLK, BLK), (KEEP * BLK) ** -0.5, 0.125, ((0, 16), (1, 16)))
    w_down = gaussian(seeds[3], (NBF, KEEP, BLK, BLK), (FF // 4) ** -0.5, 0.09375, ((0, 16), (1, 16)))
    cotangent = gaussian(seeds[4], (TOKENS, D), 1.0, 6.0, ((0, 16), (1, 16)))
    return {"tokens": tokens, "pattern": pattern, "w_up": w_up, "w_down": w_down, "cotangent": cotangent}


def activate(value):
    return jax.nn.gelu(value, approximate=True)

def scatter_blocks(terms, flat, total_rows):
    empty = jnp.zeros((total_rows, NBD, BLK), jnp.float32)
    return empty.at[:, flat].add(terms)

def round_kept(value):
    return lax.optimization_barrier(value.astype(jnp.bfloat16)).astype(jnp.float32)

def reference(tokens, pattern, w_up, w_down, cotangent):
    columns = NBF // N_MP
    total_rows = TOKENS
    token_blocks = tokens.reshape(total_rows, NBD, BLK)
    grad_blocks = cotangent.reshape(total_rows, NBD, BLK)

    def group_step(sums, group):
        out_sum, in_sum = sums
        first = (group * columns).astype(jnp.int32)
        picks = lax.dynamic_slice_in_dim(pattern, first, columns, 0)
        up_part = lax.dynamic_slice_in_dim(w_up, first, columns, 0).astype(jnp.float32)
        down_part = lax.dynamic_slice_in_dim(w_down, first, columns, 0).astype(jnp.float32)
        flat = picks.reshape(-1).astype(jnp.int32)
        token_picks = jnp.take(token_blocks, flat, axis=1).reshape(total_rows, columns, KEEP, BLK).astype(jnp.float32)
        grad_picks = jnp.take(grad_blocks, flat, axis=1).reshape(total_rows, columns, KEEP, BLK).astype(jnp.float32)
        hidden = jnp.einsum('tjkb,jkbc->tjc', token_picks, up_part)
        activated = activate(hidden).astype(jnp.bfloat16).astype(jnp.float32)
        out_terms = jnp.einsum('tjb,jkbc->tjkc', activated, down_part).reshape(total_rows, columns * KEEP, BLK)
        out_part = round_kept(scatter_blocks(out_terms, flat, total_rows))
        grad_act = jnp.einsum('tjkc,jkbc->tjb', grad_picks, down_part)
        grad_hidden = jax.vjp(activate, hidden)[1](grad_act)[0].astype(jnp.bfloat16).astype(jnp.float32)
        in_terms = jnp.einsum('tjc,jkbc->tjkb', grad_hidden, up_part).reshape(total_rows, columns * KEEP, BLK)
        in_part = round_kept(scatter_blocks(in_terms, flat, total_rows))
        token_groups = token_picks.reshape(N_DP, TOK_DEV, columns, KEEP, BLK)
        grad_groups = grad_picks.reshape(N_DP, TOK_DEV, columns, KEEP, BLK)
        hidden_groups = grad_hidden.reshape(N_DP, TOK_DEV, columns, BLK)
        act_groups = activated.reshape(N_DP, TOK_DEV, columns, BLK)
        up_grad = lax.optimization_barrier(jnp.sum(round_kept(jnp.einsum('rtjkb,rtjc->rjkbc', token_groups, hidden_groups)), axis=0))
        down_grad = lax.optimization_barrier(jnp.sum(round_kept(jnp.einsum('rtjb,rtjkc->rjkbc', act_groups, grad_groups)), axis=0))
        return ((out_sum + out_part, in_sum + in_part), (up_grad, down_grad))
    start_sums = (jnp.zeros((total_rows, NBD, BLK), jnp.float32), jnp.zeros((total_rows, NBD, BLK), jnp.float32))
    sums, grads = lax.scan(group_step, start_sums, jnp.arange(N_MP, dtype=jnp.int32))
    mixed = sums[0].reshape(total_rows, D).astype(jnp.bfloat16)
    grad_tokens = sums[1].reshape(total_rows, D).astype(jnp.bfloat16)
    grad_up = grads[0].reshape(NBF, KEEP, BLK, BLK)
    grad_down = grads[1].reshape(NBF, KEEP, BLK, BLK)
    return (mixed, grad_tokens, grad_up, grad_down)
```

```python
import jax
import jax.numpy as jnp
from jax import lax
from jax.experimental import pallas as pl
from jax.experimental.pallas import tpu as pltpu
from jax.sharding import PartitionSpec as P

AXES = ("dp", "mp")
B = 128
MIB = 1 << 20
GELU_C = 0.7978845608028654
GELU_A = 0.044715


def where_is(index):
    dp, mp = divmod(index, 16)
    return mp // 4, (dp // 8) * 2 + (mp // 2) % 2, dp % 8, mp % 2


def place_of(x, y, z, core):
    return ((y // 2) * 8 + z) * 16 + x * 4 + (y % 2) * 2 + core


def send(value, dx=0, dy=0, dz=0, dcore=0):
    pairs = []
    for source in range(256):
        x, y, z, core = where_is(source)
        target = place_of((x + dx) % 4, (y + dy) % 4, (z + dz) % 8, core ^ dcore)
        pairs.append((source, target))
    return lax.ppermute(value, AXES, pairs)


def gelu_parts(h):
    t = jnp.tanh(GELU_C * (h + GELU_A * (h * h * h)))
    half = 0.5 * (1.0 + t)
    slope = half + 0.5 * h * (1.0 - t * t) * (GELU_C * (1.0 + 3.0 * GELU_A * (h * h)))
    return h * half, slope


NT = (((1,), (1,)), ((), ()))


def dot(a, b, dims=(((1,), (0,)), ((), ()))):
    return lax.dot_general(a, b, dims, preferred_element_type=jnp.float32)


def first_kernel(spots, rows, *refs):
    x_in, g_in, w_in = refs[:8], refs[8:16], refs[16:32]
    act_out, gh_out = refs[32:34]
    grads = refs[34:50]
    xs, gs, ws, sem_x, sem_g, sem_w = refs[50:]

    def load(parts, scratch, sems, which):
        copies = []
        for n, part in enumerate(parts):
            for r in range(4):
                spot = spots[which, n * 4 + r]
                copies.append(
                    pltpu.make_async_copy(
                        part.at[r],
                        scratch.at[spot // 2, pl.ds(pl.multiple_of((spot % 2) * B, B), B)],
                        sems.at[n * 4 + r],
                    )
                )
        return copies

    copies = load(x_in, xs, sem_x, 0)
    copies += [pltpu.make_async_copy(w_in[n], ws.at[n], sem_w.at[n]) for n in range(16)]
    copies += load(g_in, gs, sem_g, 1)
    for copy in copies:
        copy.start()
    for copy in copies:
        copy.wait()

    def pick(scratch, j, s):
        p = rows[j, s]
        q = rows[j, 8 + s]
        return jnp.concatenate(
            [
                scratch[p // 4, :, pl.ds(pl.multiple_of((p % 4) * B, B), B)],
                scratch[q // 4, :, pl.ds(pl.multiple_of((q % 4) * B, B), B)],
            ],
            axis=1,
        )

    def column(j, carry):
        hidden = jnp.zeros((2 * B, B), jnp.float32)
        grad_act = jnp.zeros((2 * B, B), jnp.float32)
        for s in range(8):
            up = jnp.concatenate([ws[s, 0, j], ws[8 + s, 0, j]], axis=0)
            hidden += dot(pick(xs, j, s), up)
            down = jnp.concatenate([ws[s, 1, j], ws[8 + s, 1, j]], axis=1)
            grad_act += dot(pick(gs, j, s), down, NT)
        value, slope = gelu_parts(hidden)
        act = value.astype(jnp.bfloat16)
        gh = (slope * grad_act).astype(jnp.bfloat16)
        act_out[j] = act
        gh_out[j] = gh
        act_t = value.T.astype(jnp.bfloat16)
        gh_t = (slope * grad_act).T.astype(jnp.bfloat16)
        for s in range(8):
            up = dot(gh_t, pick(xs, j, s)).astype(jnp.bfloat16)
            grads[s][0, j] = up[:, :B]
            grads[8 + s][0, j] = up[:, B:]
            down = dot(act_t, pick(gs, j, s)).astype(jnp.bfloat16)
            grads[s][1, j] = down[:, :B]
            grads[8 + s][1, j] = down[:, B:]
        return carry

    lax.fori_loop(0, 4, column, 0)


def second_kernel(outs_at, rows, act_ref, gh_ref, *refs):
    w_in = refs[:16]
    out_refs, in_refs = refs[16], refs[17]
    ws, out_acc, in_acc, sem_w = refs[18:]
    copies = [pltpu.make_async_copy(w_in[n], ws.at[n], sem_w.at[n]) for n in range(16)]
    for copy in copies:
        copy.start()

    def clear(p, carry):
        out_acc[p] = jnp.zeros((2 * B, B), jnp.float32)
        in_acc[p] = jnp.zeros((2 * B, B), jnp.float32)
        return carry

    lax.fori_loop(0, 64, clear, 0)
    for copy in copies:
        copy.wait()

    def column(j, carry):
        act = act_ref[j]
        gh = gh_ref[j]
        for s in range(8):
            p = rows[j, s]
            q = rows[j, 8 + s]
            down = jnp.concatenate([ws[s, 1, j], ws[8 + s, 1, j]], axis=1)
            term = dot(act, down)
            out_acc[p] += term[:, :B]
            out_acc[q] += term[:, B:]
            up = jnp.concatenate([ws[s, 0, j], ws[8 + s, 0, j]], axis=0)
            term = dot(gh, up, NT)
            in_acc[p] += term[:, :B]
            in_acc[q] += term[:, B:]
        return carry

    lax.fori_loop(0, 4, column, 0)

    def finish(p, carry):
        lanes = pl.ds(pl.multiple_of((p % 4) * B, B), B)
        for half in range(2):
            rows_of = pl.ds(half * B, B)
            at = outs_at[0, p * 2 + half]
            out_refs[at // 4, at % 4, :, lanes] = out_acc[p, rows_of].astype(jnp.bfloat16)
            at = outs_at[1, p * 2 + half]
            in_refs[at // 4, at % 4, :, lanes] = in_acc[p, rows_of].astype(jnp.bfloat16)
        return carry

    lax.fori_loop(0, 64, finish, 0)


SMEM = pl.BlockSpec(memory_space=pltpu.SMEM)
VMEM = pl.BlockSpec(memory_space=pltpu.VMEM)
ANY = pl.BlockSpec(memory_space=pl.ANY)
STEPS = (0, 1, 3, 2)


def ring_of_four(value, **axis):
    ((name, _),) = axis.items()
    return [value] + [send(value, **{name: step}) for step in STEPS[1:]]


def gather_plane(shard, first, second):
    parts = jnp.stack(ring_of_four(shard, **{first: 1}))
    own = ring_of_four(parts, **{second: 1})
    return own + [send(part, dcore=1) for part in own]


def total(parts):
    value = parts[0].astype(jnp.float32)
    for part in parts[1:]:
        value = value + part.astype(jnp.float32)
    return value


def scatter_plane(parts, first, second):
    kept = []
    for n in range(4):
        kept.append(total([parts[n], send(parts[4 + n], dcore=1)]).astype(jnp.bfloat16))
    summed = [kept[0]] + [send(kept[n], **{first: STEPS[n]}) for n in (1, 2, 3)]
    summed = total(summed).astype(jnp.bfloat16)
    last = [summed[0]] + [send(summed[n], **{second: STEPS[n]}) for n in (1, 2, 3)]
    return total(last).astype(jnp.bfloat16)


def ring_gather(own, ahead, behind):
    slots = [own] + [None] * 7
    value = own
    for s in range(1, ahead + 1):
        value = send(value, dz=1)
        slots[s] = value
    value = own
    for s in range(1, behind + 1):
        value = send(value, dz=-1)
        slots[8 - s] = value
    return slots


def ring_scatter(slots, ahead, behind):
    value = slots[8 - ahead]
    for s in range(ahead - 1, 0, -1):
        value = (send(value, dz=1).astype(jnp.float32) + slots[8 - s]).astype(jnp.bfloat16)
    forward = send(value, dz=1)
    value = slots[behind]
    for s in range(behind - 1, 0, -1):
        value = (send(value, dz=-1).astype(jnp.float32) + slots[s]).astype(jnp.bfloat16)
    backward = send(value, dz=-1)
    return total([slots[0], forward, backward])


def local(tokens, pattern, w_up, w_down, cotangent):
    dp, mp = lax.axis_index("dp"), lax.axis_index("mp")
    x, y, z, core = mp // 4, (dp // 8) * 2 + (mp // 2) % 2, dp % 8, mp % 2
    yh = dp // 8
    bf16, f32 = jnp.bfloat16, jnp.float32

    steps = jnp.array(STEPS, jnp.int32)

    def spot_of(x_at, y_at, c_at):
        return (x_at * 4 + (y_at % 2) * 2 + c_at) * 2 + y_at // 2

    cores = jnp.stack([core, 1 - core])[:, None, None]
    x_first = spot_of(((x - steps) % 4)[None, None, :], ((y - steps) % 4)[None, :, None], cores)
    y_first = spot_of(((x - steps) % 4)[None, :, None], ((y - steps) % 4)[None, None, :], cores)
    spots = jnp.stack([x_first.reshape(-1), y_first.reshape(-1)]).astype(jnp.int32)
    own_rows = lax.dynamic_slice_in_dim(pattern, yh * 4, 4, 0)
    back = (z - jnp.arange(8, dtype=jnp.int32)) % 8
    rows = jnp.take(own_rows, jnp.concatenate([yh * 8 + back, (1 - yh) * 8 + back]), axis=1)
    order = jnp.array([0, 1, 3, 2], jnp.int32)
    p_all = jnp.arange(64, dtype=jnp.int32)[:, None]
    y_to = jnp.arange(2, dtype=jnp.int32)[None, :] * 2 + (p_all // 8) % 2
    x_step = order[(p_all // 16 - x) % 4] + 0 * y_to
    y_step = order[(y_to - y) % 4]
    c_step = (p_all // 4) % 2 ^ core
    out_at = (c_step * 4 + y_step) * 4 + x_step
    in_at = (c_step * 4 + x_step) * 4 + y_step
    outs_at = jnp.stack([out_at.reshape(-1), in_at.reshape(-1)]).astype(jnp.int32)

    both = jnp.stack([w_up[:, 0], w_down[:, 0]])
    piece_a = lax.dynamic_slice_in_dim(both, yh * 4, 4, 1)
    piece_b = send(lax.dynamic_slice_in_dim(both, (1 - yh) * 4, 4, 1), dy=2)
    x_parts = gather_plane(tokens, "dx", "dy")
    g_parts = gather_plane(cotangent, "dy", "dx")
    weights = ring_gather(piece_a, 4, 3) + ring_gather(piece_b, 3, 4)

    piece = jax.ShapeDtypeStruct((2, 4, B, B), bf16)
    results = pl.pallas_call(
        first_kernel,
        out_shape=[jax.ShapeDtypeStruct((4, 2 * B, B), bf16)] * 2 + [piece] * 16,
        in_specs=[SMEM, SMEM] + [ANY] * 32,
        out_specs=[VMEM] * 18,
        scratch_shapes=[
            pltpu.VMEM((16, 2 * B, 4 * B), bf16),
            pltpu.VMEM((16, 2 * B, 4 * B), bf16),
            pltpu.VMEM((16, 2, 4, B, B), bf16),
            pltpu.SemaphoreType.DMA((32,)),
            pltpu.SemaphoreType.DMA((32,)),
            pltpu.SemaphoreType.DMA((16,)),
        ],
        compiler_params=pltpu.CompilerParams(vmem_limit_bytes=30 * MIB),
        cost_estimate=pl.CostEstimate(
            flops=2_000_000_000, bytes_accessed=16 * MIB, transcendentals=0
        ),
        name="first",
    )(spots, rows, *x_parts, *g_parts, *weights)
    act, gh, grads = results[0], results[1], results[2:]

    summed_b = ring_scatter(grads[8:], 3, 4).astype(bf16)
    summed_a = ring_scatter(grads[:8], 4, 3)

    parts = jax.ShapeDtypeStruct((8, 4, B, 4 * B), bf16)
    out_parts, in_parts = pl.pallas_call(
        second_kernel,
        out_shape=[parts, parts],
        in_specs=[SMEM, SMEM, VMEM, VMEM] + [ANY] * 16,
        out_specs=[VMEM, VMEM],
        scratch_shapes=[
            pltpu.VMEM((16, 2, 4, B, B), bf16),
            pltpu.VMEM((64, 2 * B, B), f32),
            pltpu.VMEM((64, 2 * B, B), f32),
            pltpu.SemaphoreType.DMA((16,)),
        ],
        compiler_params=pltpu.CompilerParams(vmem_limit_bytes=40 * MIB),
        cost_estimate=pl.CostEstimate(
            flops=1_000_000_000, bytes_accessed=16 * MIB, transcendentals=0
        ),
        name="second",
    )(outs_at, rows, act, gh, *weights)

    mixed = scatter_plane(out_parts, "dy", "dx")
    grad_tokens = scatter_plane(in_parts, "dx", "dy")
    other = send(summed_b, dy=2).astype(f32)
    grad_both = jnp.where(
        yh == 0,
        jnp.concatenate([summed_a, other], axis=1),
        jnp.concatenate([other, summed_a], axis=1),
    )
    grad_up = jnp.swapaxes(grad_both[0], 1, 2)[:, None]
    grad_down = grad_both[1][:, None]
    return mixed, grad_tokens, grad_up, grad_down


def solution(mesh):
    return jax.shard_map(
        local,
        mesh=mesh,
        in_specs=(
            P("dp", "mp"),
            P("mp", None),
            P("mp", "dp", None, None),
            P("mp", "dp", None, None),
            P("dp", "mp"),
        ),
        out_specs=(
            P("dp", "mp"),
            P("dp", "mp"),
            P("mp", "dp", None, None),
            P("mp", "dp", None, None),
        ),
        check_vma=False,
    )
```

```python
import jax
import jax.numpy as jnp
from jax import lax
from jax.experimental import pallas as pl
from jax.experimental.pallas import tpu as pltpu
from jax.sharding import PartitionSpec as P

AXES = ("dp", "mp")
B = 128
MIB = 1 << 20
GELU_C = 0.7978845608028654
GELU_A = 0.044715


def where_is(index):
    dp, mp = divmod(index, 16)
    return mp // 4, (dp // 8) * 2 + (mp // 2) % 2, dp % 8, mp % 2


def place_of(x, y, z, core):
    return ((y // 2) * 8 + z) * 16 + x * 4 + (y % 2) * 2 + core


def send(value, step):
    return lax.ppermute(
        value, AXES, [(source, place_of(*step(*where_is(source)))) for source in range(256)]
    )


def across(steps):
    return lambda x, y, z, c: ((x + steps * (1 - c)) % 4, (y + steps * c) % 4, z, c)


def beside(steps):
    return lambda x, y, z, c: ((x + steps * c) % 4, (y + steps * (1 - c)) % 4, z, c)


def other_core(x, y, z, c):
    return x, y, z, 1 - c


def other_half(x, y, z, c):
    return x, (y + 2) % 4, z, c


def gelu_parts(h):
    t = jnp.tanh(GELU_C * (h + GELU_A * (h * h * h)))
    half = 0.5 * (1.0 + t)
    slope = half + 0.5 * h * (1.0 - t * t) * (GELU_C * (1.0 + 3.0 * GELU_A * (h * h)))
    return h * half, slope


NT = (((1,), (1,)), ((), ()))


def dot(a, b, dims=(((1,), (0,)), ((), ()))):
    return lax.dot_general(a, b, dims, preferred_element_type=jnp.float32)


def first_kernel(spots, rows, *refs):
    plane_in, w_in = refs[:8], refs[8]
    act_out, gh_out, grads = refs[9:12]
    xs, gs, ws, sem_x, sem_g, sem_w = refs[12:]

    copies = []
    for n in range(8):
        for r in range(4):
            spot = spots[n * 4 + r]
            half = pl.ds(pl.multiple_of((spot % 2) * B, B), B)
            for m, (scratch, sems) in enumerate(((xs, sem_x), (gs, sem_g))):
                copies.append(
                    pltpu.make_async_copy(
                        plane_in[n].at[r, m], scratch.at[spot // 2, half], sems.at[n * 4 + r]
                    )
                )
    copies.append(pltpu.make_async_copy(w_in, ws, sem_w))
    for copy in copies:
        copy.start()
    for copy in copies:
        copy.wait()

    def pick(scratch, j, s):
        p = rows[j, s]
        q = rows[j, 8 + s]
        return jnp.concatenate(
            [
                scratch[p // 4, :, pl.ds(pl.multiple_of((p % 4) * B, B), B)],
                scratch[q // 4, :, pl.ds(pl.multiple_of((q % 4) * B, B), B)],
            ],
            axis=1,
        )

    def column(j, carry):
        hidden = jnp.zeros((2 * B, B), jnp.float32)
        grad_act = jnp.zeros((2 * B, B), jnp.float32)
        for s in range(8):
            up = jnp.concatenate([ws[s, 0, 0, j], ws[s, 1, 0, j]], axis=0)
            hidden += dot(pick(xs, j, s), up)
            down = jnp.concatenate([ws[s, 0, 1, j], ws[s, 1, 1, j]], axis=1)
            grad_act += dot(pick(gs, j, s), down, NT)
        value, slope = gelu_parts(hidden)
        act = value.astype(jnp.bfloat16)
        gh = (slope * grad_act).astype(jnp.bfloat16)
        act_out[j] = act
        gh_out[j] = gh
        act_t = value.T.astype(jnp.bfloat16)
        gh_t = (slope * grad_act).T.astype(jnp.bfloat16)
        for s in range(8):
            up = dot(gh_t, pick(xs, j, s)).astype(jnp.bfloat16)
            grads[s, 0, 0, j] = up[:, :B]
            grads[s, 1, 0, j] = up[:, B:]
            down = dot(act_t, pick(gs, j, s)).astype(jnp.bfloat16)
            grads[s, 0, 1, j] = down[:, :B]
            grads[s, 1, 1, j] = down[:, B:]
        return carry

    lax.fori_loop(0, 4, column, 0)


def second_kernel(outs_at, rows, act_ref, gh_ref, *refs):
    w_in, parts, ws, out_acc, in_acc, sem_w = refs
    load = pltpu.make_async_copy(w_in, ws, sem_w)
    load.start()

    def clear(p, carry):
        out_acc[p] = jnp.zeros((2 * B, B), jnp.float32)
        in_acc[p] = jnp.zeros((2 * B, B), jnp.float32)
        return carry

    lax.fori_loop(0, 64, clear, 0)
    load.wait()

    def column(j, carry):
        act = act_ref[j]
        gh = gh_ref[j]
        for s in range(8):
            p = rows[j, s]
            q = rows[j, 8 + s]
            down = jnp.concatenate([ws[s, 0, 1, j], ws[s, 1, 1, j]], axis=1)
            term = dot(act, down)
            out_acc[p] += term[:, :B]
            out_acc[q] += term[:, B:]
            up = jnp.concatenate([ws[s, 0, 0, j], ws[s, 1, 0, j]], axis=0)
            term = dot(gh, up, NT)
            in_acc[p] += term[:, :B]
            in_acc[q] += term[:, B:]
        return carry

    lax.fori_loop(0, 4, column, 0)

    def finish(p, carry):
        lanes = pl.ds(pl.multiple_of((p % 4) * B, B), B)
        for half in range(2):
            rows_of = pl.ds(half * B, B)
            at = outs_at[p * 2 + half]
            parts[at // 4, at % 4, 0, :, lanes] = out_acc[p, rows_of].astype(jnp.bfloat16)
            parts[at // 4, at % 4, 1, :, lanes] = in_acc[p, rows_of].astype(jnp.bfloat16)
        return carry

    lax.fori_loop(0, 64, finish, 0)


SMEM = pl.BlockSpec(memory_space=pltpu.SMEM)
VMEM = pl.BlockSpec(memory_space=pltpu.VMEM)
ANY = pl.BlockSpec(memory_space=pl.ANY)
HALVES = [list(range(8)), list(range(8, 16))]
STEPS = (0, 1, 3, 2)


def total(parts):
    value = parts[0].astype(jnp.float32)
    for part in parts[1:]:
        value = value + part.astype(jnp.float32)
    return value


def gather_plane(shard):
    row = jnp.stack([shard] + [send(shard, across(n)) for n in STEPS[1:]])
    own = [row] + [send(row, beside(n)) for n in STEPS[1:]]
    return own + [send(part, other_core) for part in own]


def scatter_plane(parts):
    kept = [None] * 4
    for n in (3, 1, 2, 0):
        kept[n] = total([parts[n], send(parts[4 + n], other_core)]).astype(jnp.bfloat16)
    row = [kept[0]] + [send(kept[n], beside(STEPS[n])) for n in (3, 1, 2)]
    row = total(row).astype(jnp.bfloat16)
    return total([row[0]] + [send(row[n], across(STEPS[n])) for n in (3, 1, 2)]).astype(jnp.bfloat16)


def local(tokens, pattern, w_up, w_down, cotangent):
    dp, mp = lax.axis_index("dp"), lax.axis_index("mp")
    x, y, z, core = mp // 4, (dp // 8) * 2 + (mp // 2) % 2, dp % 8, mp % 2
    yh = dp // 8
    bf16, f32 = jnp.bfloat16, jnp.float32

    steps = jnp.array(STEPS, jnp.int32)
    def spots_of(c_at):
        first, second = steps[None, :], steps[:, None]
        x_at = (x - jnp.where(c_at == 0, first, second)) % 4
        y_at = (y - jnp.where(c_at == 0, second, first)) % 4
        return (x_at * 4 + (y_at % 2) * 2 + c_at) * 2 + y_at // 2

    spots = jnp.concatenate([spots_of(core).reshape(-1), spots_of(1 - core).reshape(-1)])
    spots = spots.astype(jnp.int32)
    own_rows = lax.dynamic_slice_in_dim(pattern, yh * 4, 4, 0)
    rows = jnp.where(yh == 0, own_rows, jnp.roll(own_rows, 8, axis=1))
    order = jnp.array([0, 1, 3, 2], jnp.int32)
    p_all = jnp.arange(64, dtype=jnp.int32)[:, None]
    c_to = (p_all // 4) % 2
    y_to = jnp.arange(2, dtype=jnp.int32)[None, :] * 2 + (p_all // 8) % 2
    x_step = order[(p_all // 16 - x) % 4] + 0 * y_to
    y_step = order[(y_to - y) % 4]
    first, second = jnp.where(c_to == 0, x_step, y_step), jnp.where(c_to == 0, y_step, x_step)
    outs_at = (((c_to ^ core) * 4 + second) * 4 + first).reshape(-1).astype(jnp.int32)

    both = jnp.stack([w_up[:, 0], w_down[:, 0]])
    piece_a = lax.dynamic_slice_in_dim(both, yh * 4, 4, 1)
    piece_b = lax.dynamic_slice_in_dim(both, (1 - yh) * 4, 4, 1)
    plane = gather_plane(jnp.stack([tokens, cotangent]))
    weights = lax.all_gather(
        jnp.stack([piece_a, send(piece_b, other_half)]), "dp", axis_index_groups=HALVES
    )

    act, gh, grads = pl.pallas_call(
        first_kernel,
        out_shape=[jax.ShapeDtypeStruct((4, 2 * B, B), bf16)] * 2
        + [jax.ShapeDtypeStruct((8, 2, 2, 4, B, B), bf16)],
        in_specs=[SMEM, SMEM] + [ANY] * 9,
        out_specs=[VMEM] * 3,
        scratch_shapes=[
            pltpu.VMEM((16, 2 * B, 4 * B), bf16),
            pltpu.VMEM((16, 2 * B, 4 * B), bf16),
            pltpu.VMEM((8, 2, 2, 4, B, B), bf16),
            pltpu.SemaphoreType.DMA((32,)),
            pltpu.SemaphoreType.DMA((32,)),
            pltpu.SemaphoreType.DMA,
        ],
        compiler_params=pltpu.CompilerParams(vmem_limit_bytes=18 * MIB),
        cost_estimate=pl.CostEstimate(
            flops=2_000_000_000, bytes_accessed=16 * MIB, transcendentals=0
        ),
        name="first",
    )(spots, rows, *plane, weights)
    summed = lax.psum_scatter(
        grads, "dp", scatter_dimension=0, axis_index_groups=HALVES, tiled=True
    )[0]

    parts = pl.pallas_call(
        second_kernel,
        out_shape=jax.ShapeDtypeStruct((8, 4, 2, B, 4 * B), bf16),
        in_specs=[SMEM, SMEM, VMEM, VMEM, ANY],
        out_specs=VMEM,
        scratch_shapes=[
            pltpu.VMEM((8, 2, 2, 4, B, B), bf16),
            pltpu.VMEM((64, 2 * B, B), f32),
            pltpu.VMEM((64, 2 * B, B), f32),
            pltpu.SemaphoreType.DMA,
        ],
        compiler_params=pltpu.CompilerParams(vmem_limit_bytes=24 * MIB),
        cost_estimate=pl.CostEstimate(
            flops=1_000_000_000, bytes_accessed=16 * MIB, transcendentals=0
        ),
        name="second",
    )(outs_at, rows, act, gh, weights)

    result = scatter_plane(parts)
    mixed, grad_tokens = result[0], result[1]
    other = send(summed[1], other_half).astype(f32)
    summed_a = summed[0].astype(f32)
    grad_both = jnp.where(
        yh == 0,
        jnp.concatenate([summed_a, other], axis=1),
        jnp.concatenate([other, summed_a], axis=1),
    )
    grad_up = jnp.swapaxes(grad_both[0], 1, 2)[:, None]
    grad_down = grad_both[1][:, None]
    return mixed, grad_tokens, grad_up, grad_down


def solution(mesh):
    return jax.shard_map(
        local,
        mesh=mesh,
        in_specs=(
            P("dp", "mp"),
            P("mp", None),
            P("mp", "dp", None, None),
            P("mp", "dp", None, None),
            P("dp", "mp"),
        ),
        out_specs=(
            P("dp", "mp"),
            P("dp", "mp"),
            P("mp", "dp", None, None),
            P("mp", "dp", None, None),
        ),
        check_vma=False,
    )
```

```python
import jax
import jax.numpy as jnp
from jax import lax
from jax.experimental import pallas as pl
from jax.experimental.pallas import tpu as pltpu
from jax.sharding import PartitionSpec as P

AXES = ("dp", "mp")
B = 128
MIB = 1 << 20
GELU_C = 0.7978845608028654
GELU_A = 0.044715


def where_is(index):
    dp, mp = divmod(index, 16)
    return mp // 4, (dp // 8) * 2 + (mp // 2) % 2, dp % 8, mp % 2


def place_of(x, y, z, core):
    return ((y // 2) * 8 + z) * 16 + x * 4 + (y % 2) * 2 + core


def send(value, step):
    return lax.ppermute(
        value, AXES, [(source, place_of(*step(*where_is(source)))) for source in range(256)]
    )


def across(steps):
    return lambda x, y, z, c: ((x + steps * (1 - c)) % 4, (y + steps * c) % 4, z, c)


def beside(steps):
    return lambda x, y, z, c: ((x + steps * c) % 4, (y + steps * (1 - c)) % 4, z, c)


def other_core(x, y, z, c):
    return x, y, z, 1 - c


def other_half(x, y, z, c):
    return x, (y + 2) % 4, z, c


def gelu_parts(h):
    t = jnp.tanh(GELU_C * (h + GELU_A * (h * h * h)))
    half = 0.5 * (1.0 + t)
    slope = half + 0.5 * h * (1.0 - t * t) * (GELU_C * (1.0 + 3.0 * GELU_A * (h * h)))
    return h * half, slope


NT = (((1,), (1,)), ((), ()))


def dot(a, b, dims=(((1,), (0,)), ((), ()))):
    return lax.dot_general(a, b, dims, preferred_element_type=jnp.float32)


def place_kernel(spots, *refs):
    parts, x_out, g_out = refs[:8], refs[8], refs[9]
    xs, gs, sem_x, sem_g, sem_out = refs[10:]
    copies = ([], [])
    for m, (scratch, sems) in enumerate(((xs, sem_x), (gs, sem_g))):
        for n in range(8):
            for r in range(4):
                spot = spots[n * 4 + r]
                half = pl.ds(pl.multiple_of((spot % 2) * B, B), B)
                copies[m].append(
                    pltpu.make_async_copy(
                        parts[n].at[r, m], scratch.at[spot // 2, half], sems.at[n * 4 + r]
                    )
                )
    for copy in copies[0] + copies[1]:
        copy.start()
    stores = (
        pltpu.make_async_copy(xs, x_out, sem_out.at[0]),
        pltpu.make_async_copy(gs, g_out, sem_out.at[1]),
    )
    for m in range(2):
        for copy in copies[m]:
            copy.wait()
        stores[m].start()
    for store in stores:
        store.wait()


def first_kernel(rows, x_in, g_in, w_in, act_out, gh_out, grads_out, *scratch):
    xs, gs, ws, grads, sem_x, sem_g, sem_in, sem_out = scratch

    def store(j):
        return pltpu.make_async_copy(grads.at[j], grads_out.at[:, :, :, j], sem_out.at[j])

    def load_w(j):
        return pltpu.make_async_copy(w_in.at[:, :, :, j], ws.at[j], sem_in.at[j])

    def load(j):
        for source, target, sems in ((x_in, xs, sem_x), (g_in, gs, sem_g)):
            for s in range(8):
                for half in range(2):
                    p = rows[j, half * 8 + s]
                    lanes = pl.ds(pl.multiple_of((p % 4) * B, B), B)
                    pltpu.make_async_copy(
                        source.at[p // 4, :, lanes], target.at[j, s, half], sems.at[j]
                    ).start()
        load_w(j).start()

    def pick(scratch, j, s):
        return jnp.concatenate([scratch[j, s, 0], scratch[j, s, 1]], axis=1)

    def column(j, carry):
        pl.when(j < 3)(lambda: load(j + 1))
        for target, sems in ((xs, sem_x), (gs, sem_g)):
            pltpu.make_async_copy(target.at[j], target.at[j], sems.at[j]).wait()
        load_w(j).wait()
        hidden = jnp.zeros((2 * B, B), jnp.float32)
        grad_act = jnp.zeros((2 * B, B), jnp.float32)
        for s in range(8):
            up = jnp.concatenate([ws[j, s, 0, 0], ws[j, s, 1, 0]], axis=0)
            hidden += dot(pick(xs, j, s), up)
            down = jnp.concatenate([ws[j, s, 0, 1], ws[j, s, 1, 1]], axis=1)
            grad_act += dot(pick(gs, j, s), down, NT)
        value, slope = gelu_parts(hidden)
        grad_hidden = slope * grad_act
        act_out[j] = value.astype(jnp.bfloat16)
        gh_out[j] = grad_hidden.astype(jnp.bfloat16)
        act_t = value.T.astype(jnp.bfloat16)
        gh_t = grad_hidden.T.astype(jnp.bfloat16)
        for s in range(8):
            up = dot(gh_t, pick(xs, j, s)).astype(jnp.bfloat16)
            grads[j, s, 0, 0] = up[:, :B]
            grads[j, s, 1, 0] = up[:, B:]
            down = dot(act_t, pick(gs, j, s)).astype(jnp.bfloat16)
            grads[j, s, 0, 1] = down[:, :B]
            grads[j, s, 1, 1] = down[:, B:]
        store(j).start()
        return carry

    load(0)
    lax.fori_loop(0, 4, column, 0)
    for j in range(4):
        store(j).wait()


def second_kernel(outs_at, rows, act_ref, gh_ref, *refs):
    w_in, parts, ws, out_acc, in_acc, sem_w = refs

    def load(j):
        return pltpu.make_async_copy(w_in.at[:, :, :, j], ws.at[j], sem_w.at[j])

    for j in range(4):
        load(j).start()

    def clear(p, carry):
        out_acc[p] = jnp.zeros((2 * B, B), jnp.float32)
        in_acc[p] = jnp.zeros((2 * B, B), jnp.float32)
        return carry

    lax.fori_loop(0, 64, clear, 0)

    def column(j, carry):
        load(j).wait()
        act = act_ref[j]
        gh = gh_ref[j]
        for s in range(8):
            p = rows[j, s]
            q = rows[j, 8 + s]
            down = jnp.concatenate([ws[j, s, 0, 1], ws[j, s, 1, 1]], axis=1)
            term = dot(act, down)
            out_acc[p] += term[:, :B]
            out_acc[q] += term[:, B:]
            up = jnp.concatenate([ws[j, s, 0, 0], ws[j, s, 1, 0]], axis=0)
            term = dot(gh, up, NT)
            in_acc[p] += term[:, :B]
            in_acc[q] += term[:, B:]
        return carry

    lax.fori_loop(0, 4, column, 0)

    def finish(p, carry):
        lanes = pl.ds(pl.multiple_of((p % 4) * B, B), B)
        for half in range(2):
            rows_of = pl.ds(half * B, B)
            at = outs_at[p * 2 + half]
            parts[at // 4, at % 4, 0, :, lanes] = out_acc[p, rows_of].astype(jnp.bfloat16)
            parts[at // 4, at % 4, 1, :, lanes] = in_acc[p, rows_of].astype(jnp.bfloat16)
        return carry

    lax.fori_loop(0, 64, finish, 0)


SMEM = pl.BlockSpec(memory_space=pltpu.SMEM)
VMEM = pl.BlockSpec(memory_space=pltpu.VMEM)
ANY = pl.BlockSpec(memory_space=pl.ANY)
HBM = pl.BlockSpec(memory_space=pltpu.HBM)
HALVES = [list(range(8)), list(range(8, 16))]
STEPS = (0, 1, 3, 2)


def total(parts):
    value = parts[0].astype(jnp.float32)
    for part in parts[1:]:
        value = value + part.astype(jnp.float32)
    return value


def gather_plane(shard):
    row = jnp.stack([shard] + [send(shard, across(n)) for n in STEPS[1:]])
    own = [row] + [send(row, beside(n)) for n in STEPS[1:]]
    return own + [send(part, other_core) for part in own]


def scatter_plane(parts):
    kept = [None] * 4
    for n in (3, 1, 2, 0):
        kept[n] = total([parts[n], send(parts[4 + n], other_core)]).astype(jnp.bfloat16)
    row = [kept[0]] + [send(kept[n], beside(STEPS[n])) for n in (3, 1, 2)]
    row = total(row).astype(jnp.bfloat16)
    return total([row[0]] + [send(row[n], across(STEPS[n])) for n in (3, 1, 2)]).astype(jnp.bfloat16)


def local(tokens, pattern, w_up, w_down, cotangent):
    dp, mp = lax.axis_index("dp"), lax.axis_index("mp")
    x, y, z, core = mp // 4, (dp // 8) * 2 + (mp // 2) % 2, dp % 8, mp % 2
    yh = dp // 8
    bf16, f32 = jnp.bfloat16, jnp.float32

    steps = jnp.array(STEPS, jnp.int32)
    def spots_of(c_at):
        first, second = steps[None, :], steps[:, None]
        x_at = (x - jnp.where(c_at == 0, first, second)) % 4
        y_at = (y - jnp.where(c_at == 0, second, first)) % 4
        return (x_at * 4 + (y_at % 2) * 2 + c_at) * 2 + y_at // 2

    spots = jnp.concatenate([spots_of(core).reshape(-1), spots_of(1 - core).reshape(-1)])
    spots = spots.astype(jnp.int32)
    own_rows = lax.dynamic_slice_in_dim(pattern, yh * 4, 4, 0)
    rows = jnp.where(yh == 0, own_rows, jnp.roll(own_rows, 8, axis=1))
    order = jnp.array([0, 1, 3, 2], jnp.int32)
    p_all = jnp.arange(64, dtype=jnp.int32)[:, None]
    c_to = (p_all // 4) % 2
    y_to = jnp.arange(2, dtype=jnp.int32)[None, :] * 2 + (p_all // 8) % 2
    x_step = order[(p_all // 16 - x) % 4] + 0 * y_to
    y_step = order[(y_to - y) % 4]
    first, second = jnp.where(c_to == 0, x_step, y_step), jnp.where(c_to == 0, y_step, x_step)
    outs_at = (((c_to ^ core) * 4 + second) * 4 + first).reshape(-1).astype(jnp.int32)

    both = jnp.stack([w_up[:, 0], w_down[:, 0]])
    piece_a = lax.dynamic_slice_in_dim(both, yh * 4, 4, 1)
    piece_b = lax.dynamic_slice_in_dim(both, (1 - yh) * 4, 4, 1)
    other_b = send(piece_b, other_half)
    plane = gather_plane(jnp.stack([tokens, cotangent]))
    weights = lax.all_gather(
        jnp.stack([piece_a, other_b]), "dp", axis_index_groups=HALVES
    )

    gathered = jax.ShapeDtypeStruct((16, 2 * B, 4 * B), bf16)
    xs, gs = pl.pallas_call(
        place_kernel,
        out_shape=[gathered] * 2,
        in_specs=[SMEM] + [ANY] * 8,
        out_specs=[HBM] * 2,
        scratch_shapes=[
            pltpu.VMEM((16, 2 * B, 4 * B), bf16),
            pltpu.VMEM((16, 2 * B, 4 * B), bf16),
            pltpu.SemaphoreType.DMA((32,)),
            pltpu.SemaphoreType.DMA((32,)),
            pltpu.SemaphoreType.DMA((2,)),
        ],
        compiler_params=pltpu.CompilerParams(vmem_limit_bytes=56 * MIB),
        cost_estimate=pl.CostEstimate(flops=0, bytes_accessed=16 * MIB, transcendentals=0),
        name="place",
    )(spots, *plane)
    act, gh, grads = pl.pallas_call(
        first_kernel,
        out_shape=[jax.ShapeDtypeStruct((4, 2 * B, B), bf16)] * 2
        + [jax.ShapeDtypeStruct((8, 2, 2, 4, B, B), bf16)],
        in_specs=[SMEM, HBM, HBM, HBM],
        out_specs=[VMEM, VMEM, HBM],
        scratch_shapes=[
            pltpu.VMEM((4, 8, 2, 2 * B, B), bf16),
            pltpu.VMEM((4, 8, 2, 2 * B, B), bf16),
            pltpu.VMEM((4, 8, 2, 2, B, B), bf16),
            pltpu.VMEM((4, 8, 2, 2, B, B), bf16),
            pltpu.SemaphoreType.DMA((4,)),
            pltpu.SemaphoreType.DMA((4,)),
            pltpu.SemaphoreType.DMA((4,)),
            pltpu.SemaphoreType.DMA((4,)),
        ],
        compiler_params=pltpu.CompilerParams(vmem_limit_bytes=58 * MIB),
        cost_estimate=pl.CostEstimate(
            flops=2_000_000_000, bytes_accessed=16 * MIB, transcendentals=0
        ),
        name="first",
    )(rows, xs, gs, weights)

    summed = lax.psum_scatter(
        grads, "dp", scatter_dimension=0, axis_index_groups=HALVES, tiled=True
    )[0]

    parts = pl.pallas_call(
        second_kernel,
        out_shape=jax.ShapeDtypeStruct((8, 4, 2, B, 4 * B), bf16),
        in_specs=[SMEM, SMEM, VMEM, VMEM, HBM],
        out_specs=VMEM,
        scratch_shapes=[
            pltpu.VMEM((4, 8, 2, 2, B, B), bf16),
            pltpu.VMEM((64, 2 * B, B), f32),
            pltpu.VMEM((64, 2 * B, B), f32),
            pltpu.SemaphoreType.DMA((4,)),
        ],
        compiler_params=pltpu.CompilerParams(vmem_limit_bytes=24 * MIB),
        cost_estimate=pl.CostEstimate(
            flops=1_000_000_000, bytes_accessed=16 * MIB, transcendentals=0
        ),
        name="second",
    )(outs_at, rows, act, gh, weights)

    result = scatter_plane(parts)
    mixed, grad_tokens = result[0], result[1]
    other = send(summed[1], other_half).astype(f32)
    summed_a = summed[0].astype(f32)
    grad_both = jnp.where(
        yh == 0,
        jnp.concatenate([summed_a, other], axis=1),
        jnp.concatenate([other, summed_a], axis=1),
    )
    grad_up = jnp.swapaxes(grad_both[0], 1, 2)[:, None]
    grad_down = grad_both[1][:, None]
    return mixed, grad_tokens, grad_up, grad_down


def solution(mesh):
    return jax.shard_map(
        local,
        mesh=mesh,
        in_specs=(
            P("dp", "mp"),
            P("mp", None),
            P("mp", "dp", None, None),
            P("mp", "dp", None, None),
            P("dp", "mp"),
        ),
        out_specs=(
            P("dp", "mp"),
            P("dp", "mp"),
            P("mp", "dp", None, None),
            P("mp", "dp", None, None),
        ),
        check_vma=False,
    )
```

```python
import jax
import jax.numpy as jnp
from jax import lax
from jax.experimental import pallas as pl
from jax.experimental.pallas import tpu as pltpu
from jax.sharding import PartitionSpec as P

AXES = ("dp", "mp")
B = 128
MIB = 1 << 20
GELU_C = 0.7978845608028654
GELU_A = 0.044715


def where_is(index):
    dp, mp = divmod(index, 16)
    return mp // 4, (dp // 8) * 2 + (mp // 2) % 2, dp % 8, mp % 2


def place_of(x, y, z, core):
    return ((y // 2) * 8 + z) * 16 + x * 4 + (y % 2) * 2 + core


def send(value, step):
    return lax.ppermute(
        value, AXES, [(source, place_of(*step(*where_is(source)))) for source in range(256)]
    )


def across(steps):
    return lambda x, y, z, c: ((x + steps * (1 - c)) % 4, (y + steps * c) % 4, z, c)


def beside(steps):
    return lambda x, y, z, c: ((x + steps * c) % 4, (y + steps * (1 - c)) % 4, z, c)


def other_core(x, y, z, c):
    return x, y, z, 1 - c


def other_half(x, y, z, c):
    return x, (y + 2) % 4, z, c


def gelu_parts(h):
    t = jnp.tanh(GELU_C * (h + GELU_A * (h * h * h)))
    half = 0.5 * (1.0 + t)
    slope = half + 0.5 * h * (1.0 - t * t) * (GELU_C * (1.0 + 3.0 * GELU_A * (h * h)))
    return h * half, slope


NT = (((1,), (1,)), ((), ()))


def dot(a, b, dims=(((1,), (0,)), ((), ()))):
    return lax.dot_general(a, b, dims, preferred_element_type=jnp.float32)


def place_kernel(spots, *refs):
    parts, x_out, g_out = refs[:8], refs[8], refs[9]
    xs, gs, sem_x, sem_g, sem_out = refs[10:]
    copies = ([], [])
    for m, (scratch, sems) in enumerate(((xs, sem_x), (gs, sem_g))):
        for n in range(8):
            for r in range(4):
                spot = spots[n * 4 + r]
                half = pl.ds(pl.multiple_of((spot % 2) * B, B), B)
                copies[m].append(
                    pltpu.make_async_copy(
                        parts[n].at[r, m], scratch.at[spot // 2, half], sems.at[n * 4 + r]
                    )
                )
    for copy in copies[0] + copies[1]:
        copy.start()
    stores = (
        pltpu.make_async_copy(xs, x_out, sem_out.at[0]),
        pltpu.make_async_copy(gs, g_out, sem_out.at[1]),
    )
    for m in range(2):
        for copy in copies[m]:
            copy.wait()
        stores[m].start()
    for store in stores:
        store.wait()


def first_kernel(rows, x_in, g_in, w_in, act_out, gh_out, grads_out, *scratch):
    xs, gs, ws, grads, sem_x, sem_g, sem_in, sem_out = scratch

    def store(j):
        return pltpu.make_async_copy(grads.at[j], grads_out.at[:, :, :, j], sem_out.at[j])

    def load_w(j):
        return pltpu.make_async_copy(w_in.at[:, :, :, j], ws.at[j], sem_in.at[j])

    def load(j):
        for source, target, sems in ((x_in, xs, sem_x), (g_in, gs, sem_g)):
            for s in range(8):
                for half in range(2):
                    p = rows[j, half * 8 + s]
                    lanes = pl.ds(pl.multiple_of((p % 4) * B, B), B)
                    pltpu.make_async_copy(
                        source.at[p // 4, :, lanes], target.at[j, s, half], sems.at[j]
                    ).start()
        load_w(j).start()

    def pick(scratch, j, s):
        return jnp.concatenate([scratch[j, s, 0], scratch[j, s, 1]], axis=1)

    def column(j, carry):
        pl.when(j < 3)(lambda: load(j + 1))
        for target, sems in ((xs, sem_x), (gs, sem_g)):
            pltpu.make_async_copy(target.at[j], target.at[j], sems.at[j]).wait()
        load_w(j).wait()
        hidden = jnp.zeros((2 * B, B), jnp.float32)
        grad_act = jnp.zeros((2 * B, B), jnp.float32)
        for s in range(8):
            up = jnp.concatenate([ws[j, s, 0, 0], ws[j, s, 1, 0]], axis=0)
            hidden += dot(pick(xs, j, s), up)
            down = jnp.concatenate([ws[j, s, 0, 1], ws[j, s, 1, 1]], axis=1)
            grad_act += dot(pick(gs, j, s), down, NT)
        value, slope = gelu_parts(hidden)
        grad_hidden = slope * grad_act
        act_out[j] = value.astype(jnp.bfloat16)
        gh_out[j] = grad_hidden.astype(jnp.bfloat16)
        act_t = value.T.astype(jnp.bfloat16)
        gh_t = grad_hidden.T.astype(jnp.bfloat16)
        for s in range(8):
            up = dot(gh_t, pick(xs, j, s)).astype(jnp.bfloat16)
            grads[j, s, 0, 0] = up[:, :B]
            grads[j, s, 1, 0] = up[:, B:]
            down = dot(act_t, pick(gs, j, s)).astype(jnp.bfloat16)
            grads[j, s, 0, 1] = down[:, :B]
            grads[j, s, 1, 1] = down[:, B:]
        store(j).start()
        return carry

    load(0)
    lax.fori_loop(0, 4, column, 0)
    for j in range(4):
        store(j).wait()


def second_kernel(outs_at, rows, act_ref, gh_ref, *refs):
    w_in, parts, ws, out_acc, in_acc, sem_w = refs

    def load(j):
        return pltpu.make_async_copy(w_in.at[:, :, :, j], ws.at[j], sem_w.at[j])

    for j in range(4):
        load(j).start()

    def clear(p, carry):
        out_acc[p] = jnp.zeros((2 * B, B), jnp.float32)
        in_acc[p] = jnp.zeros((2 * B, B), jnp.float32)
        return carry

    lax.fori_loop(0, 64, clear, 0)

    def column(j, carry):
        load(j).wait()
        act = act_ref[j]
        gh = gh_ref[j]
        for s in range(8):
            p = rows[j, s]
            q = rows[j, 8 + s]
            down = jnp.concatenate([ws[j, s, 0, 1], ws[j, s, 1, 1]], axis=1)
            term = dot(act, down)
            out_acc[p] += term[:, :B]
            out_acc[q] += term[:, B:]
            up = jnp.concatenate([ws[j, s, 0, 0], ws[j, s, 1, 0]], axis=0)
            term = dot(gh, up, NT)
            in_acc[p] += term[:, :B]
            in_acc[q] += term[:, B:]
        return carry

    lax.fori_loop(0, 4, column, 0)

    def finish(p, carry):
        lanes = pl.ds(pl.multiple_of((p % 4) * B, B), B)
        for half in range(2):
            rows_of = pl.ds(half * B, B)
            at = outs_at[p * 2 + half]
            parts[at // 4, at % 4, 0, :, lanes] = out_acc[p, rows_of].astype(jnp.bfloat16)
            parts[at // 4, at % 4, 1, :, lanes] = in_acc[p, rows_of].astype(jnp.bfloat16)
        return carry

    lax.fori_loop(0, 64, finish, 0)


SMEM = pl.BlockSpec(memory_space=pltpu.SMEM)
VMEM = pl.BlockSpec(memory_space=pltpu.VMEM)
ANY = pl.BlockSpec(memory_space=pl.ANY)
HBM = pl.BlockSpec(memory_space=pltpu.HBM)
HALVES = [list(range(8)), list(range(8, 16))]
STEPS = (0, 1, 3, 2)


def total(parts):
    value = parts[0].astype(jnp.float32)
    for part in parts[1:]:
        value = value + part.astype(jnp.float32)
    return value


def gather_plane(shard):
    row = jnp.stack([shard] + [send(shard, across(n)) for n in STEPS[1:]])
    own = [row] + [send(row, beside(n)) for n in STEPS[1:]]
    return own + [send(part, other_core) for part in own]


def scatter_plane(parts):
    kept = [None] * 4
    for n in (3, 1, 2, 0):
        kept[n] = total([parts[n], send(parts[4 + n], other_core)]).astype(jnp.bfloat16)
    row = [kept[0]] + [send(kept[n], beside(STEPS[n])) for n in (3, 1, 2)]
    row = total(row).astype(jnp.bfloat16)
    return [row[0]] + [send(row[n], across(STEPS[n])) for n in (3, 1, 2)]


def local(tokens, pattern, w_up, w_down, cotangent):
    dp, mp = lax.axis_index("dp"), lax.axis_index("mp")
    x, y, z, core = mp // 4, (dp // 8) * 2 + (mp // 2) % 2, dp % 8, mp % 2
    yh = dp // 8
    bf16, f32 = jnp.bfloat16, jnp.float32

    steps = jnp.array(STEPS, jnp.int32)
    def spots_of(c_at):
        first, second = steps[None, :], steps[:, None]
        x_at = (x - jnp.where(c_at == 0, first, second)) % 4
        y_at = (y - jnp.where(c_at == 0, second, first)) % 4
        return (x_at * 4 + (y_at % 2) * 2 + c_at) * 2 + y_at // 2

    spots = jnp.concatenate([spots_of(core).reshape(-1), spots_of(1 - core).reshape(-1)])
    spots = spots.astype(jnp.int32)
    own_rows = lax.dynamic_slice_in_dim(pattern, yh * 4, 4, 0)
    rows = jnp.where(yh == 0, own_rows, jnp.roll(own_rows, 8, axis=1))
    order = jnp.array([0, 1, 3, 2], jnp.int32)
    p_all = jnp.arange(64, dtype=jnp.int32)[:, None]
    c_to = (p_all // 4) % 2
    y_to = jnp.arange(2, dtype=jnp.int32)[None, :] * 2 + (p_all // 8) % 2
    x_step = order[(p_all // 16 - x) % 4] + 0 * y_to
    y_step = order[(y_to - y) % 4]
    first, second = jnp.where(c_to == 0, x_step, y_step), jnp.where(c_to == 0, y_step, x_step)
    outs_at = (((c_to ^ core) * 4 + second) * 4 + first).reshape(-1).astype(jnp.int32)

    both = jnp.stack([w_up[:, 0], w_down[:, 0]])
    other_b = send(lax.dynamic_slice_in_dim(both, (1 - yh) * 4, 4, 1), other_half)
    both = jnp.stack(lax.optimization_barrier((w_up[:, 0], w_down[:, 0])))
    piece_a = lax.dynamic_slice_in_dim(both, yh * 4, 4, 1)
    plane = gather_plane(jnp.stack([tokens, cotangent]))
    weights = lax.all_gather(
        jnp.stack([piece_a, other_b]), "dp", axis_index_groups=HALVES
    )

    gathered = jax.ShapeDtypeStruct((16, 2 * B, 4 * B), bf16)
    xs, gs = pl.pallas_call(
        place_kernel,
        out_shape=[gathered] * 2,
        in_specs=[SMEM] + [ANY] * 8,
        out_specs=[HBM] * 2,
        scratch_shapes=[
            pltpu.VMEM((16, 2 * B, 4 * B), bf16),
            pltpu.VMEM((16, 2 * B, 4 * B), bf16),
            pltpu.SemaphoreType.DMA((32,)),
            pltpu.SemaphoreType.DMA((32,)),
            pltpu.SemaphoreType.DMA((2,)),
        ],
        compiler_params=pltpu.CompilerParams(vmem_limit_bytes=56 * MIB),
        cost_estimate=pl.CostEstimate(flops=0, bytes_accessed=16 * MIB, transcendentals=0),
        name="place",
    )(spots, *plane)
    act, gh, grads = pl.pallas_call(
        first_kernel,
        out_shape=[jax.ShapeDtypeStruct((4, 2 * B, B), bf16)] * 2
        + [jax.ShapeDtypeStruct((8, 2, 2, 4, B, B), bf16)],
        in_specs=[SMEM, HBM, HBM, HBM],
        out_specs=[VMEM, VMEM, HBM],
        scratch_shapes=[
            pltpu.VMEM((4, 8, 2, 2 * B, B), bf16),
            pltpu.VMEM((4, 8, 2, 2 * B, B), bf16),
            pltpu.VMEM((4, 8, 2, 2, B, B), bf16),
            pltpu.VMEM((4, 8, 2, 2, B, B), bf16),
            pltpu.SemaphoreType.DMA((4,)),
            pltpu.SemaphoreType.DMA((4,)),
            pltpu.SemaphoreType.DMA((4,)),
            pltpu.SemaphoreType.DMA((4,)),
        ],
        compiler_params=pltpu.CompilerParams(vmem_limit_bytes=58 * MIB),
        cost_estimate=pl.CostEstimate(
            flops=2_000_000_000, bytes_accessed=16 * MIB, transcendentals=0
        ),
        name="first",
    )(rows, xs, gs, weights)

    summed = lax.psum_scatter(
        grads, "dp", scatter_dimension=0, axis_index_groups=HALVES, tiled=True
    )[0]

    parts = pl.pallas_call(
        second_kernel,
        out_shape=jax.ShapeDtypeStruct((8, 4, 2, B, 4 * B), bf16),
        in_specs=[SMEM, SMEM, VMEM, VMEM, HBM],
        out_specs=VMEM,
        scratch_shapes=[
            pltpu.VMEM((4, 8, 2, 2, B, B), bf16),
            pltpu.VMEM((64, 2 * B, B), f32),
            pltpu.VMEM((64, 2 * B, B), f32),
            pltpu.SemaphoreType.DMA((4,)),
        ],
        compiler_params=pltpu.CompilerParams(vmem_limit_bytes=24 * MIB),
        cost_estimate=pl.CostEstimate(
            flops=1_000_000_000, bytes_accessed=16 * MIB, transcendentals=0
        ),
        name="second",
    )(outs_at, rows, act, gh, weights)

    last = scatter_plane(parts)
    other = send(jnp.stack([jnp.swapaxes(summed[1, 0], 1, 2), summed[1, 1]]), other_half)
    own, last = lax.optimization_barrier((summed[0], last))
    own = jnp.stack([jnp.swapaxes(own[0], 1, 2), own[1]])
    grads = jnp.where(
        yh == 0, jnp.concatenate([own, other], axis=1), jnp.concatenate([other, own], axis=1)
    ).astype(f32)
    grad_up, grad_down = grads[0][:, None], grads[1][:, None]
    result = total(last).astype(bf16)
    mixed, grad_tokens = result[0], result[1]
    return mixed, grad_tokens, grad_up, grad_down


def solution(mesh):
    return jax.shard_map(
        local,
        mesh=mesh,
        in_specs=(
            P("dp", "mp"),
            P("mp", None),
            P("mp", "dp", None, None),
            P("mp", "dp", None, None),
            P("dp", "mp"),
        ),
        out_specs=(
            P("dp", "mp"),
            P("dp", "mp"),
            P("mp", "dp", None, None),
            P("mp", "dp", None, None),
        ),
        check_vma=False,
    )
```

```python
import jax
import jax.numpy as jnp
from jax import lax
from jax.experimental import pallas as pl
from jax.experimental.pallas import tpu as pltpu
from jax.sharding import PartitionSpec as P

AXES = ("dp", "mp")
B = 128
MIB = 1 << 20
GELU_C = 0.7978845608028654
GELU_A = 0.044715


def where_is(index):
    dp, mp = divmod(index, 16)
    return mp // 4, (dp // 8) * 2 + (mp // 2) % 2, dp % 8, mp % 2


def place_of(x, y, z, core):
    return ((y // 2) * 8 + z) * 16 + x * 4 + (y % 2) * 2 + core


def send(value, step):
    return lax.ppermute(
        value, AXES, [(source, place_of(*step(*where_is(source)))) for source in range(256)]
    )


def across(steps):
    return lambda x, y, z, c: ((x + steps * (1 - c)) % 4, (y + steps * c) % 4, z, c)


def beside(steps):
    return lambda x, y, z, c: ((x + steps * c) % 4, (y + steps * (1 - c)) % 4, z, c)


def other_core(x, y, z, c):
    return x, y, z, 1 - c


def other_half(x, y, z, c):
    return x, (y + 2) % 4, z, c


def gelu_parts(h):
    t = jnp.tanh(GELU_C * (h + GELU_A * (h * h * h)))
    half = 0.5 * (1.0 + t)
    slope = half + 0.5 * h * (1.0 - t * t) * (GELU_C * (1.0 + 3.0 * GELU_A * (h * h)))
    return h * half, slope


NT = (((1,), (1,)), ((), ()))


def dot(a, b, dims=(((1,), (0,)), ((), ()))):
    return lax.dot_general(a, b, dims, preferred_element_type=jnp.float32)


def place_kernel(spots, *refs):
    parts, x_out, g_out = refs[:8], refs[8], refs[9]
    xs, gs, sem_x, sem_g, sem_out = refs[10:]
    copies = ([], [])
    for m, (scratch, sems) in enumerate(((xs, sem_x), (gs, sem_g))):
        for n in range(8):
            for r in range(4):
                spot = spots[n * 4 + r]
                half = pl.ds(pl.multiple_of((spot % 2) * B, B), B)
                copies[m].append(
                    pltpu.make_async_copy(
                        parts[n].at[r, m], scratch.at[spot // 2, half], sems.at[n * 4 + r]
                    )
                )
    for copy in copies[0] + copies[1]:
        copy.start()
    stores = (
        pltpu.make_async_copy(xs, x_out, sem_out.at[0]),
        pltpu.make_async_copy(gs, g_out, sem_out.at[1]),
    )
    for m in range(2):
        for copy in copies[m]:
            copy.wait()
        stores[m].start()
    for store in stores:
        store.wait()


def first_kernel(rows, x_in, g_in, w_in, act_out, gh_out, grads_out, *scratch):
    xs, gs, ws, grads, sem_x, sem_g, sem_in, sem_out = scratch

    def store(j):
        return pltpu.make_async_copy(grads.at[j], grads_out.at[:, :, :, j], sem_out.at[j])

    def load_w(j):
        return pltpu.make_async_copy(w_in.at[:, :, :, j], ws.at[j], sem_in.at[j])

    def load(j):
        for source, target, sems in ((x_in, xs, sem_x), (g_in, gs, sem_g)):
            for s in range(8):
                for half in range(2):
                    p = rows[j, half * 8 + s]
                    lanes = pl.ds(pl.multiple_of((p % 4) * B, B), B)
                    pltpu.make_async_copy(
                        source.at[p // 4, :, lanes], target.at[j, s, half], sems.at[j]
                    ).start()
        load_w(j).start()

    def pick(scratch, j, s):
        return jnp.concatenate([scratch[j, s, 0], scratch[j, s, 1]], axis=1)

    def two_columns(i, carry):
        pl.when(i < 1)(lambda: [load(2), load(3)] and None)
        pair = (2 * i, 2 * i + 1)
        for j in pair:
            for target, sems in ((xs, sem_x), (gs, sem_g)):
                pltpu.make_async_copy(target.at[j], target.at[j], sems.at[j]).wait()
            load_w(j).wait()
        hidden = [jnp.zeros((2 * B, B), jnp.float32)] * 2
        grad_act = [jnp.zeros((2 * B, B), jnp.float32)] * 2
        for s in range(8):
            for n, j in enumerate(pair):
                up = jnp.concatenate([ws[j, s, 0, 0], ws[j, s, 1, 0]], axis=0)
                hidden[n] += dot(pick(xs, j, s), up)
                down = jnp.concatenate([ws[j, s, 0, 1], ws[j, s, 1, 1]], axis=1)
                grad_act[n] += dot(pick(gs, j, s), down, NT)
        turned = []
        for n, j in enumerate(pair):
            value, slope = gelu_parts(hidden[n])
            grad_hidden = slope * grad_act[n]
            act_out[j] = value.astype(jnp.bfloat16)
            gh_out[j] = grad_hidden.astype(jnp.bfloat16)
            turned.append((value.T.astype(jnp.bfloat16), grad_hidden.T.astype(jnp.bfloat16)))
        for n, j in enumerate(pair):
            act_t, gh_t = turned[n]
            for s in range(8):
                up = dot(gh_t, pick(xs, j, s)).astype(jnp.bfloat16)
                grads[j, s, 0, 0] = up[:, :B]
                grads[j, s, 1, 0] = up[:, B:]
                down = dot(act_t, pick(gs, j, s)).astype(jnp.bfloat16)
                grads[j, s, 0, 1] = down[:, :B]
                grads[j, s, 1, 1] = down[:, B:]
            store(j).start()
        return carry

    load(0)
    load(1)
    lax.fori_loop(0, 2, two_columns, 0)
    for j in range(4):
        store(j).wait()


def second_kernel(outs_at, rows, act_ref, gh_ref, *refs):
    w_in, parts, ws, out_acc, in_acc, sem_w = refs

    def load(j):
        return pltpu.make_async_copy(w_in.at[:, :, :, j], ws.at[j], sem_w.at[j])

    for j in range(4):
        load(j).start()

    def clear(p, carry):
        out_acc[p] = jnp.zeros((2 * B, B), jnp.float32)
        in_acc[p] = jnp.zeros((2 * B, B), jnp.float32)
        return carry

    lax.fori_loop(0, 64, clear, 0)

    def column(j, carry):
        load(j).wait()
        act = act_ref[j]
        gh = gh_ref[j]
        for s in range(8):
            p = rows[j, s]
            q = rows[j, 8 + s]
            down = jnp.concatenate([ws[j, s, 0, 1], ws[j, s, 1, 1]], axis=1)
            term = dot(act, down)
            out_acc[p] += term[:, :B]
            out_acc[q] += term[:, B:]
            up = jnp.concatenate([ws[j, s, 0, 0], ws[j, s, 1, 0]], axis=0)
            term = dot(gh, up, NT)
            in_acc[p] += term[:, :B]
            in_acc[q] += term[:, B:]
        return carry

    lax.fori_loop(0, 4, column, 0)

    def finish(p, carry):
        lanes = pl.ds(pl.multiple_of((p % 4) * B, B), B)
        for half in range(2):
            rows_of = pl.ds(half * B, B)
            at = outs_at[p * 2 + half]
            parts[at // 4, at % 4, 0, :, lanes] = out_acc[p, rows_of].astype(jnp.bfloat16)
            parts[at // 4, at % 4, 1, :, lanes] = in_acc[p, rows_of].astype(jnp.bfloat16)
        return carry

    lax.fori_loop(0, 64, finish, 0)


SMEM = pl.BlockSpec(memory_space=pltpu.SMEM)
VMEM = pl.BlockSpec(memory_space=pltpu.VMEM)
ANY = pl.BlockSpec(memory_space=pl.ANY)
HBM = pl.BlockSpec(memory_space=pltpu.HBM)
HALVES = [list(range(8)), list(range(8, 16))]
STEPS = (0, 1, 3, 2)


def total(parts):
    value = parts[0].astype(jnp.float32)
    for part in parts[1:]:
        value = value + part.astype(jnp.float32)
    return value


def gather_plane(shard):
    row = jnp.stack([shard] + [send(shard, across(n)) for n in STEPS[1:]])
    own = [row] + [send(row, beside(n)) for n in STEPS[1:]]
    return own + [send(part, other_core) for part in own]


def scatter_plane(parts):
    kept = [None] * 4
    for n in (3, 1, 2, 0):
        kept[n] = total([parts[n], send(parts[4 + n], other_core)]).astype(jnp.bfloat16)
    row = [kept[0]] + [send(kept[n], beside(STEPS[n])) for n in (3, 1, 2)]
    row = total(row).astype(jnp.bfloat16)
    return [row[0]] + [send(row[n], across(STEPS[n])) for n in (3, 1, 2)]


def local(tokens, pattern, w_up, w_down, cotangent):
    dp, mp = lax.axis_index("dp"), lax.axis_index("mp")
    x, y, z, core = mp // 4, (dp // 8) * 2 + (mp // 2) % 2, dp % 8, mp % 2
    yh = dp // 8
    bf16, f32 = jnp.bfloat16, jnp.float32

    steps = jnp.array(STEPS, jnp.int32)
    def spots_of(c_at):
        first, second = steps[None, :], steps[:, None]
        x_at = (x - jnp.where(c_at == 0, first, second)) % 4
        y_at = (y - jnp.where(c_at == 0, second, first)) % 4
        return (x_at * 4 + (y_at % 2) * 2 + c_at) * 2 + y_at // 2

    spots = jnp.concatenate([spots_of(core).reshape(-1), spots_of(1 - core).reshape(-1)])
    spots = spots.astype(jnp.int32)
    own_rows = lax.dynamic_slice_in_dim(pattern, yh * 4, 4, 0)
    rows = jnp.where(yh == 0, own_rows, jnp.roll(own_rows, 8, axis=1))
    order = jnp.array([0, 1, 3, 2], jnp.int32)
    p_all = jnp.arange(64, dtype=jnp.int32)[:, None]
    c_to = (p_all // 4) % 2
    y_to = jnp.arange(2, dtype=jnp.int32)[None, :] * 2 + (p_all // 8) % 2
    x_step = order[(p_all // 16 - x) % 4] + 0 * y_to
    y_step = order[(y_to - y) % 4]
    first, second = jnp.where(c_to == 0, x_step, y_step), jnp.where(c_to == 0, y_step, x_step)
    outs_at = (((c_to ^ core) * 4 + second) * 4 + first).reshape(-1).astype(jnp.int32)

    both = jnp.stack([w_up[:, 0], w_down[:, 0]])
    other_b = send(lax.dynamic_slice_in_dim(both, (1 - yh) * 4, 4, 1), other_half)
    both = jnp.stack(lax.optimization_barrier((w_up[:, 0], w_down[:, 0])))
    piece_a = lax.dynamic_slice_in_dim(both, yh * 4, 4, 1)
    plane = gather_plane(jnp.stack([tokens, cotangent]))
    weights = lax.all_gather(
        jnp.stack([piece_a, other_b]), "dp", axis_index_groups=HALVES
    )

    gathered = jax.ShapeDtypeStruct((16, 2 * B, 4 * B), bf16)
    xs, gs = pl.pallas_call(
        place_kernel,
        out_shape=[gathered] * 2,
        in_specs=[SMEM] + [ANY] * 8,
        out_specs=[HBM] * 2,
        scratch_shapes=[
            pltpu.VMEM((16, 2 * B, 4 * B), bf16),
            pltpu.VMEM((16, 2 * B, 4 * B), bf16),
            pltpu.SemaphoreType.DMA((32,)),
            pltpu.SemaphoreType.DMA((32,)),
            pltpu.SemaphoreType.DMA((2,)),
        ],
        compiler_params=pltpu.CompilerParams(vmem_limit_bytes=56 * MIB),
        cost_estimate=pl.CostEstimate(flops=0, bytes_accessed=16 * MIB, transcendentals=0),
        name="place",
    )(spots, *plane)
    act, gh, grads = pl.pallas_call(
        first_kernel,
        out_shape=[jax.ShapeDtypeStruct((4, 2 * B, B), bf16)] * 2
        + [jax.ShapeDtypeStruct((8, 2, 2, 4, B, B), bf16)],
        in_specs=[SMEM, HBM, HBM, HBM],
        out_specs=[VMEM, VMEM, HBM],
        scratch_shapes=[
            pltpu.VMEM((4, 8, 2, 2 * B, B), bf16),
            pltpu.VMEM((4, 8, 2, 2 * B, B), bf16),
            pltpu.VMEM((4, 8, 2, 2, B, B), bf16),
            pltpu.VMEM((4, 8, 2, 2, B, B), bf16),
            pltpu.SemaphoreType.DMA((4,)),
            pltpu.SemaphoreType.DMA((4,)),
            pltpu.SemaphoreType.DMA((4,)),
            pltpu.SemaphoreType.DMA((4,)),
        ],
        compiler_params=pltpu.CompilerParams(vmem_limit_bytes=58 * MIB),
        cost_estimate=pl.CostEstimate(
            flops=2_000_000_000, bytes_accessed=16 * MIB, transcendentals=0
        ),
        name="first",
    )(rows, xs, gs, weights)

    summed = lax.psum_scatter(
        grads, "dp", scatter_dimension=0, axis_index_groups=HALVES, tiled=True
    )[0]

    parts = pl.pallas_call(
        second_kernel,
        out_shape=jax.ShapeDtypeStruct((8, 4, 2, B, 4 * B), bf16),
        in_specs=[SMEM, SMEM, VMEM, VMEM, HBM],
        out_specs=VMEM,
        scratch_shapes=[
            pltpu.VMEM((4, 8, 2, 2, B, B), bf16),
            pltpu.VMEM((64, 2 * B, B), f32),
            pltpu.VMEM((64, 2 * B, B), f32),
            pltpu.SemaphoreType.DMA((4,)),
        ],
        compiler_params=pltpu.CompilerParams(vmem_limit_bytes=24 * MIB),
        cost_estimate=pl.CostEstimate(
            flops=1_000_000_000, bytes_accessed=16 * MIB, transcendentals=0
        ),
        name="second",
    )(outs_at, rows, act, gh, weights)

    last = scatter_plane(parts)
    other = send(jnp.stack([jnp.swapaxes(summed[1, 0], 1, 2), summed[1, 1]]), other_half)
    own = lax.optimization_barrier(summed[0])
    own = jnp.stack([jnp.swapaxes(own[0], 1, 2), own[1]])
    grads = jnp.where(
        yh == 0, jnp.concatenate([own, other], axis=1), jnp.concatenate([other, own], axis=1)
    ).astype(f32)
    grad_up, grad_down = grads[0][:, None], grads[1][:, None]
    last, grad_up = lax.optimization_barrier((last, grad_up))
    result = total(last).astype(bf16)
    mixed, grad_tokens = result[0], result[1]
    return mixed, grad_tokens, grad_up, grad_down


def solution(mesh):
    return jax.shard_map(
        local,
        mesh=mesh,
        in_specs=(
            P("dp", "mp"),
            P("mp", None),
            P("mp", "dp", None, None),
            P("mp", "dp", None, None),
            P("dp", "mp"),
        ),
        out_specs=(
            P("dp", "mp"),
            P("dp", "mp"),
            P("mp", "dp", None, None),
            P("mp", "dp", None, None),
        ),
        check_vma=False,
    )
```

```python
import jax
import jax.numpy as jnp
from jax import lax
from jax.experimental import pallas as pl
from jax.experimental.pallas import tpu as pltpu
from jax.sharding import PartitionSpec as P

AXES = ("dp", "mp")
B = 128
MIB = 1 << 20
GELU_C = 0.7978845608028654
GELU_A = 0.044715


def where_is(index):
    dp, mp = divmod(index, 16)
    return mp // 4, (dp // 8) * 2 + (mp // 2) % 2, dp % 8, mp % 2


def place_of(x, y, z, core):
    return ((y // 2) * 8 + z) * 16 + x * 4 + (y % 2) * 2 + core


def send(value, step):
    return lax.ppermute(
        value, AXES, [(source, place_of(*step(*where_is(source)))) for source in range(256)]
    )


def across(steps):
    return lambda x, y, z, c: ((x + steps * (1 - c)) % 4, (y + steps * c) % 4, z, c)


def beside(steps):
    return lambda x, y, z, c: ((x + steps * c) % 4, (y + steps * (1 - c)) % 4, z, c)


def other_core(x, y, z, c):
    return x, y, z, 1 - c


def other_half(x, y, z, c):
    return x, (y + 2) % 4, z, c


def gelu_parts(h):
    t = jnp.tanh(GELU_C * (h + GELU_A * (h * h * h)))
    half = 0.5 * (1.0 + t)
    slope = half + 0.5 * h * (1.0 - t * t) * (GELU_C * (1.0 + 3.0 * GELU_A * (h * h)))
    return h * half, slope


NT = (((1,), (1,)), ((), ()))


def dot(a, b, dims=(((1,), (0,)), ((), ()))):
    return lax.dot_general(a, b, dims, preferred_element_type=jnp.float32)


def place_kernel(spots, *refs):
    parts, x_out, g_out = refs[:8], refs[8], refs[9]
    xs, gs, sem_x, sem_g, sem_out = refs[10:]
    copies = ([], [])
    for m, (scratch, sems) in enumerate(((xs, sem_x), (gs, sem_g))):
        for n in range(8):
            for r in range(4):
                spot = spots[n * 4 + r]
                half = pl.ds(pl.multiple_of((spot % 2) * B, B), B)
                copies[m].append(
                    pltpu.make_async_copy(
                        parts[n].at[r, m], scratch.at[spot // 2, half], sems.at[n * 4 + r]
                    )
                )
    for copy in copies[0] + copies[1]:
        copy.start()
    stores = (
        pltpu.make_async_copy(xs, x_out, sem_out.at[0]),
        pltpu.make_async_copy(gs, g_out, sem_out.at[1]),
    )
    for m in range(2):
        for copy in copies[m]:
            copy.wait()
        stores[m].start()
    for store in stores:
        store.wait()


def first_kernel(rows_in, x_in, g_in, w_in, act_out, gh_out, grads_out, *scratch):
    xs, gs, ws, grads, rows, sem_x, sem_g, sem_in, sem_out, sem_rows = scratch

    def store(j, half):
        slots = pl.ds(4 * half, 4)
        return pltpu.make_async_copy(
            grads.at[j, slots], grads_out.at[slots, :, :, j], sem_out.at[j, half]
        )

    def load_w(j):
        return pltpu.make_async_copy(w_in.at[:, :, :, j], ws.at[j], sem_in.at[j])

    def load(j):
        for source, target, sems in ((x_in, xs, sem_x), (g_in, gs, sem_g)):
            for s in range(8):
                for half in range(2):
                    p = rows[j, half * 8 + s]
                    lanes = pl.ds(pl.multiple_of((p % 4) * B, B), B)
                    pltpu.make_async_copy(
                        source.at[p // 4, :, lanes], target.at[j, s, half], sems.at[j]
                    ).start()

    def pick(scratch, j, s):
        return jnp.concatenate([scratch[j, s, 0], scratch[j, s, 1]], axis=1)

    def two_columns(i, carry):
        @pl.when(i < 1)
        def _():
            for j in (2, 3):
                load_w(j).start()
                load(j)

        pair = (2 * i, 2 * i + 1)
        for j in pair:
            for target, sems in ((xs, sem_x), (gs, sem_g)):
                pltpu.make_async_copy(target.at[j], target.at[j], sems.at[j]).wait()
            load_w(j).wait()
        hidden = [jnp.zeros((2 * B, B), jnp.float32)] * 2
        grad_act = [jnp.zeros((2 * B, B), jnp.float32)] * 2
        for s in range(8):
            for n, j in enumerate(pair):
                up = jnp.concatenate([ws[j, s, 0, 0], ws[j, s, 1, 0]], axis=0)
                hidden[n] += dot(pick(xs, j, s), up)
                down = jnp.concatenate([ws[j, s, 0, 1], ws[j, s, 1, 1]], axis=1)
                grad_act[n] += dot(pick(gs, j, s), down, NT)
        turned = []
        for n, j in enumerate(pair):
            value, slope = gelu_parts(hidden[n])
            grad_hidden = slope * grad_act[n]
            act_out[j] = value.astype(jnp.bfloat16)
            gh_out[j] = grad_hidden.astype(jnp.bfloat16)
            turned.append((value.T.astype(jnp.bfloat16), grad_hidden.T.astype(jnp.bfloat16)))
        for n, j in enumerate(pair):
            act_t, gh_t = turned[n]
            for s in range(8):
                up = dot(gh_t, pick(xs, j, s)).astype(jnp.bfloat16)
                grads[j, s, 0, 0] = up[:, :B]
                grads[j, s, 1, 0] = up[:, B:]
                down = dot(act_t, pick(gs, j, s)).astype(jnp.bfloat16)
                grads[j, s, 0, 1] = down[:, :B]
                grads[j, s, 1, 1] = down[:, B:]
                if s % 4 == 3:
                    store(j, s // 4).start()
        return carry

    fetch = pltpu.make_async_copy(rows_in, rows, sem_rows)
    fetch.start()
    for j in (0, 1):
        load_w(j).start()
    fetch.wait()
    for j in (0, 1):
        load(j)
    lax.fori_loop(0, 2, two_columns, 0)
    for j in range(4):
        for half in range(2):
            store(j, half).wait()


def second_kernel(outs_at, rows, act_ref, gh_ref, *refs):
    w_in, parts, ws, out_acc, in_acc, sem_w = refs

    def load(j):
        return pltpu.make_async_copy(w_in.at[:, :, :, j], ws.at[j], sem_w.at[j])

    for j in range(4):
        load(j).start()

    def clear(p, carry):
        out_acc[p] = jnp.zeros((2 * B, B), jnp.float32)
        in_acc[p] = jnp.zeros((2 * B, B), jnp.float32)
        return carry

    lax.fori_loop(0, 64, clear, 0)

    def column(j, carry):
        load(j).wait()
        act = act_ref[j]
        gh = gh_ref[j]
        for s in range(8):
            p = rows[j, s]
            q = rows[j, 8 + s]
            down = jnp.concatenate([ws[j, s, 0, 1], ws[j, s, 1, 1]], axis=1)
            term = dot(act, down)
            out_acc[p] += term[:, :B]
            out_acc[q] += term[:, B:]
            up = jnp.concatenate([ws[j, s, 0, 0], ws[j, s, 1, 0]], axis=0)
            term = dot(gh, up, NT)
            in_acc[p] += term[:, :B]
            in_acc[q] += term[:, B:]
        return carry

    lax.fori_loop(0, 4, column, 0)

    def finish(p, carry):
        lanes = pl.ds(pl.multiple_of((p % 4) * B, B), B)
        for half in range(2):
            rows_of = pl.ds(half * B, B)
            at = outs_at[p * 2 + half]
            parts[at // 4, at % 4, 0, :, lanes] = out_acc[p, rows_of].astype(jnp.bfloat16)
            parts[at // 4, at % 4, 1, :, lanes] = in_acc[p, rows_of].astype(jnp.bfloat16)
        return carry

    lax.fori_loop(0, 64, finish, 0)


SMEM = pl.BlockSpec(memory_space=pltpu.SMEM)
VMEM = pl.BlockSpec(memory_space=pltpu.VMEM)
ANY = pl.BlockSpec(memory_space=pl.ANY)
HBM = pl.BlockSpec(memory_space=pltpu.HBM)
HALVES = [list(range(8)), list(range(8, 16))]
STEPS = (0, 1, 3, 2)


def total(parts):
    value = parts[0].astype(jnp.float32)
    for part in parts[1:]:
        value = value + part.astype(jnp.float32)
    return value


def gather_plane(shard):
    row = jnp.stack([shard] + [send(shard, across(n)) for n in STEPS[1:]])
    own = [row] + [send(row, beside(n)) for n in STEPS[1:]]
    return own + [send(part, other_core) for part in own]


def scatter_plane(parts):
    kept = [None] * 4
    for n in (3, 1, 2, 0):
        kept[n] = total([parts[n], send(parts[4 + n], other_core)]).astype(jnp.bfloat16)
    row = [kept[0]] + [send(kept[n], beside(STEPS[n])) for n in (3, 1, 2)]
    row = total(row).astype(jnp.bfloat16)
    return [row[0]] + [send(row[n], across(STEPS[n])) for n in (3, 1, 2)]


def local(tokens, pattern, w_up, w_down, cotangent):
    dp, mp = lax.axis_index("dp"), lax.axis_index("mp")
    x, y, z, core = mp // 4, (dp // 8) * 2 + (mp // 2) % 2, dp % 8, mp % 2
    yh = dp // 8
    bf16, f32 = jnp.bfloat16, jnp.float32

    steps = jnp.array(STEPS, jnp.int32)
    def spots_of(c_at):
        first, second = steps[None, :], steps[:, None]
        x_at = (x - jnp.where(c_at == 0, first, second)) % 4
        y_at = (y - jnp.where(c_at == 0, second, first)) % 4
        return (x_at * 4 + (y_at % 2) * 2 + c_at) * 2 + y_at // 2

    spots = jnp.concatenate([spots_of(core).reshape(-1), spots_of(1 - core).reshape(-1)])
    spots = spots.astype(jnp.int32)
    own_rows = lax.dynamic_slice_in_dim(pattern, yh * 4, 4, 0)
    rows = jnp.where(yh == 0, own_rows, jnp.roll(own_rows, 8, axis=1))
    order = jnp.array([0, 1, 3, 2], jnp.int32)
    p_all = jnp.arange(64, dtype=jnp.int32)[:, None]
    c_to = (p_all // 4) % 2
    y_to = jnp.arange(2, dtype=jnp.int32)[None, :] * 2 + (p_all // 8) % 2
    x_step = order[(p_all // 16 - x) % 4] + 0 * y_to
    y_step = order[(y_to - y) % 4]
    first, second = jnp.where(c_to == 0, x_step, y_step), jnp.where(c_to == 0, y_step, x_step)
    outs_at = (((c_to ^ core) * 4 + second) * 4 + first).reshape(-1).astype(jnp.int32)

    both = jnp.stack([w_up[:, 0], w_down[:, 0]])
    other_b = send(lax.dynamic_slice_in_dim(both, (1 - yh) * 4, 4, 1), other_half)
    both = jnp.stack(lax.optimization_barrier((w_up[:, 0], w_down[:, 0])))
    piece_a = lax.dynamic_slice_in_dim(both, yh * 4, 4, 1)
    plane = gather_plane(jnp.stack([tokens, cotangent]))
    weights = lax.all_gather(
        jnp.stack([piece_a, other_b]), "dp", axis_index_groups=HALVES
    )

    gathered = jax.ShapeDtypeStruct((16, 2 * B, 4 * B), bf16)
    xs, gs = pl.pallas_call(
        place_kernel,
        out_shape=[gathered] * 2,
        in_specs=[SMEM] + [ANY] * 8,
        out_specs=[HBM] * 2,
        scratch_shapes=[
            pltpu.VMEM((16, 2 * B, 4 * B), bf16),
            pltpu.VMEM((16, 2 * B, 4 * B), bf16),
            pltpu.SemaphoreType.DMA((32,)),
            pltpu.SemaphoreType.DMA((32,)),
            pltpu.SemaphoreType.DMA((2,)),
        ],
        compiler_params=pltpu.CompilerParams(vmem_limit_bytes=56 * MIB),
        cost_estimate=pl.CostEstimate(flops=0, bytes_accessed=16 * MIB, transcendentals=0),
        name="place",
    )(spots, *plane)
    act, gh, grads = pl.pallas_call(
        first_kernel,
        out_shape=[jax.ShapeDtypeStruct((4, 2 * B, B), bf16)] * 2
        + [jax.ShapeDtypeStruct((8, 2, 2, 4, B, B), bf16)],
        in_specs=[HBM, HBM, HBM, HBM],
        out_specs=[VMEM, VMEM, HBM],
        scratch_shapes=[
            pltpu.VMEM((4, 8, 2, 2 * B, B), bf16),
            pltpu.VMEM((4, 8, 2, 2 * B, B), bf16),
            pltpu.VMEM((4, 8, 2, 2, B, B), bf16),
            pltpu.VMEM((4, 8, 2, 2, B, B), bf16),
            pltpu.SMEM((4, 16), jnp.int32),
            pltpu.SemaphoreType.DMA((4,)),
            pltpu.SemaphoreType.DMA((4,)),
            pltpu.SemaphoreType.DMA((4,)),
            pltpu.SemaphoreType.DMA((4, 2)),
            pltpu.SemaphoreType.DMA,
        ],
        compiler_params=pltpu.CompilerParams(vmem_limit_bytes=58 * MIB),
        cost_estimate=pl.CostEstimate(
            flops=2_000_000_000, bytes_accessed=16 * MIB, transcendentals=0
        ),
        name="first",
    )(rows, xs, gs, weights)

    summed = lax.psum_scatter(
        grads, "dp", scatter_dimension=0, axis_index_groups=HALVES, tiled=True
    )[0]

    parts = pl.pallas_call(
        second_kernel,
        out_shape=jax.ShapeDtypeStruct((8, 4, 2, B, 4 * B), bf16),
        in_specs=[SMEM, SMEM, VMEM, VMEM, HBM],
        out_specs=VMEM,
        scratch_shapes=[
            pltpu.VMEM((4, 8, 2, 2, B, B), bf16),
            pltpu.VMEM((64, 2 * B, B), f32),
            pltpu.VMEM((64, 2 * B, B), f32),
            pltpu.SemaphoreType.DMA((4,)),
        ],
        compiler_params=pltpu.CompilerParams(vmem_limit_bytes=24 * MIB),
        cost_estimate=pl.CostEstimate(
            flops=1_000_000_000, bytes_accessed=16 * MIB, transcendentals=0
        ),
        name="second",
    )(outs_at, rows, act, gh, weights)

    last = scatter_plane(parts)
    other = send(jnp.stack([jnp.swapaxes(summed[1, 0], 1, 2), summed[1, 1]]), other_half)
    own = lax.optimization_barrier(summed[0])
    own = jnp.stack([jnp.swapaxes(own[0], 1, 2), own[1]])
    grads = jnp.where(
        yh == 0, jnp.concatenate([own, other], axis=1), jnp.concatenate([other, own], axis=1)
    ).astype(f32)
    grad_up, grad_down = grads[0][:, None], grads[1][:, None]
    last, grad_up = lax.optimization_barrier((last, grad_up))
    result = total(last).astype(bf16)
    mixed, grad_tokens = result[0], result[1]
    return mixed, grad_tokens, grad_up, grad_down


def solution(mesh):
    return jax.shard_map(
        local,
        mesh=mesh,
        in_specs=(
            P("dp", "mp"),
            P("mp", None),
            P("mp", "dp", None, None),
            P("mp", "dp", None, None),
            P("dp", "mp"),
        ),
        out_specs=(
            P("dp", "mp"),
            P("dp", "mp"),
            P("mp", "dp", None, None),
            P("mp", "dp", None, None),
        ),
        check_vma=False,
    )
```

```python
import jax
import jax.numpy as jnp
from jax import lax
from jax.experimental import pallas as pl
from jax.experimental.pallas import tpu as pltpu
from jax.sharding import PartitionSpec as P

AXES = ("dp", "mp")
B = 128
MIB = 1 << 20
GELU_C = 0.7978845608028654
GELU_A = 0.044715


def where_is(index):
    dp, mp = divmod(index, 16)
    return mp // 4, (dp // 8) * 2 + (mp // 2) % 2, dp % 8, mp % 2


def place_of(x, y, z, core):
    return ((y // 2) * 8 + z) * 16 + x * 4 + (y % 2) * 2 + core


def send(value, step):
    return lax.ppermute(
        value, AXES, [(source, place_of(*step(*where_is(source)))) for source in range(256)]
    )


def across(steps):
    return lambda x, y, z, c: ((x + steps * (1 - c)) % 4, (y + steps * c) % 4, z, c)


def beside(steps):
    return lambda x, y, z, c: ((x + steps * c) % 4, (y + steps * (1 - c)) % 4, z, c)


def other_core(x, y, z, c):
    return x, y, z, 1 - c


def other_half(x, y, z, c):
    return x, (y + 2) % 4, z, c


def gelu_parts(h):
    t = jnp.tanh(GELU_C * (h + GELU_A * (h * h * h)))
    half = 0.5 * (1.0 + t)
    slope = half + 0.5 * h * (1.0 - t * t) * (GELU_C * (1.0 + 3.0 * GELU_A * (h * h)))
    return h * half, slope


NT = (((1,), (1,)), ((), ()))


def dot(a, b, dims=(((1,), (0,)), ((), ()))):
    return lax.dot_general(a, b, dims, preferred_element_type=jnp.float32)


def place_kernel(spots, *refs):
    parts, x_out, g_out = refs[:8], refs[8], refs[9]
    xs, gs, sem_x, sem_g, sem_out = refs[10:]
    copies = ([], [])
    for m, (scratch, sems) in enumerate(((xs, sem_x), (gs, sem_g))):
        for n in range(8):
            for r in range(4):
                spot = spots[n * 4 + r]
                half = pl.ds(pl.multiple_of((spot % 2) * B, B), B)
                copies[m].append(
                    pltpu.make_async_copy(
                        parts[n].at[r, m], scratch.at[spot // 2, half], sems.at[n * 4 + r]
                    )
                )
    for copy in copies[0] + copies[1]:
        copy.start()
    stores = (
        pltpu.make_async_copy(xs, x_out, sem_out.at[0]),
        pltpu.make_async_copy(gs, g_out, sem_out.at[1]),
    )
    for m in range(2):
        for copy in copies[m]:
            copy.wait()
        stores[m].start()
    for store in stores:
        store.wait()


def first_kernel(rows_in, x_in, g_in, w_in, act_out, gh_out, grads_out, *scratch):
    xs, gs, ws, grads, rows, sem_x, sem_g, sem_in, sem_out, sem_rows = scratch

    def store(j, half):
        slots = pl.ds(4 * half, 4)
        return pltpu.make_async_copy(
            grads.at[j, slots], grads_out.at[slots, :, :, j], sem_out.at[j, half]
        )

    def load_w(j):
        return pltpu.make_async_copy(w_in.at[:, :, :, j], ws.at[j], sem_in.at[j])

    def load(j):
        for source, target, sems in ((x_in, xs, sem_x), (g_in, gs, sem_g)):
            for s in range(8):
                for half in range(2):
                    p = rows[j, half * 8 + s]
                    lanes = pl.ds(pl.multiple_of((p % 4) * B, B), B)
                    pltpu.make_async_copy(
                        source.at[p // 4, :, lanes], target.at[j, s, half], sems.at[j]
                    ).start()

    def pick(scratch, j, s):
        return jnp.concatenate([scratch[j, s, 0], scratch[j, s, 1]], axis=1)

    def two_columns(i, carry):
        @pl.when(i < 1)
        def _():
            for j in (2, 3):
                load_w(j).start()
                load(j)

        pair = (2 * i, 2 * i + 1)
        for j in pair:
            for target, sems in ((xs, sem_x), (gs, sem_g)):
                pltpu.make_async_copy(target.at[j], target.at[j], sems.at[j]).wait()
            load_w(j).wait()
        hidden = [jnp.zeros((2 * B, B), jnp.float32)] * 2
        grad_act = [jnp.zeros((2 * B, B), jnp.float32)] * 2
        for s in range(8):
            for n, j in enumerate(pair):
                up = jnp.concatenate([ws[j, s, 0, 0], ws[j, s, 1, 0]], axis=0)
                hidden[n] += dot(pick(xs, j, s), up)
                down = jnp.concatenate([ws[j, s, 0, 1], ws[j, s, 1, 1]], axis=1)
                grad_act[n] += dot(pick(gs, j, s), down, NT)
        turned = []
        for n, j in enumerate(pair):
            value, slope = gelu_parts(hidden[n])
            grad_hidden = slope * grad_act[n]
            act_out[j] = value.astype(jnp.bfloat16)
            gh_out[j] = grad_hidden.astype(jnp.bfloat16)
            turned.append((value.T.astype(jnp.bfloat16), grad_hidden.T.astype(jnp.bfloat16)))
        for n, j in enumerate(pair):
            act_t, gh_t = turned[n]
            for s in range(8):
                up = dot(gh_t, pick(xs, j, s)).astype(jnp.bfloat16)
                grads[j, s, 0, 0] = up[:, :B]
                grads[j, s, 1, 0] = up[:, B:]
                down = dot(act_t, pick(gs, j, s)).astype(jnp.bfloat16)
                grads[j, s, 0, 1] = down[:, :B]
                grads[j, s, 1, 1] = down[:, B:]
                if s % 4 == 3:
                    store(j, s // 4).start()
        return carry

    fetch = pltpu.make_async_copy(rows_in, rows, sem_rows)
    fetch.start()
    for j in (0, 1):
        load_w(j).start()
    fetch.wait()
    for j in (0, 1):
        load(j)
    lax.fori_loop(0, 2, two_columns, 0)
    for j in range(4):
        for half in range(2):
            store(j, half).wait()


def second_kernel(outs_at, rows, act_ref, gh_ref, *refs):
    w_in, parts = refs[0], refs[1:9]
    ws, out_acc, in_acc, stage, sem_w, sem_out = refs[9:]

    def load(j):
        return pltpu.make_async_copy(w_in.at[:, :, :, j], ws.at[j], sem_w.at[j])

    for j in range(4):
        load(j).start()

    def clear(p, carry):
        out_acc[p] = jnp.zeros((2 * B, B), jnp.float32)
        in_acc[p] = jnp.zeros((2 * B, B), jnp.float32)
        return carry

    lax.fori_loop(0, 64, clear, 0)

    def two_columns(i, carry):
        pair = (2 * i, 2 * i + 1)
        for j in pair:
            load(j).wait()
        for s in range(8):
            terms = []
            for j in pair:
                down = jnp.concatenate([ws[j, s, 0, 1], ws[j, s, 1, 1]], axis=1)
                up = jnp.concatenate([ws[j, s, 0, 0], ws[j, s, 1, 0]], axis=0)
                terms.append((dot(act_ref[j], down), dot(gh_ref[j], up, NT)))
            for j, (out_term, in_term) in zip(pair, terms):
                for half in range(2):
                    p = rows[j, half * 8 + s]
                    out_acc[p] += out_term[:, half * B : (half + 1) * B]
                    in_acc[p] += in_term[:, half * B : (half + 1) * B]
        return carry

    lax.fori_loop(0, 2, two_columns, 0)

    def finish(m, carry):
        for half in range(2):
            rows_of = pl.ds(half * B, B)
            for n in range(4):
                lanes = pl.ds(n * B, B)
                stage[m, half, 0, :, lanes] = out_acc[m * 4 + n, rows_of].astype(jnp.bfloat16)
                stage[m, half, 1, :, lanes] = in_acc[m * 4 + n, rows_of].astype(jnp.bfloat16)
            at = outs_at[m * 8 + half]
            for n, part in enumerate(parts):

                @pl.when(at // 4 == n)
                def _(part=part):
                    pltpu.make_async_copy(stage.at[m, half], part.at[at % 4], sem_out).start()

        return carry

    lax.fori_loop(0, 16, finish, 0)
    pltpu.make_async_copy(stage, stage, sem_out).wait()


SMEM = pl.BlockSpec(memory_space=pltpu.SMEM)
VMEM = pl.BlockSpec(memory_space=pltpu.VMEM)
ANY = pl.BlockSpec(memory_space=pl.ANY)
HBM = pl.BlockSpec(memory_space=pltpu.HBM)
HALVES = [list(range(8)), list(range(8, 16))]
STEPS = (0, 1, 3, 2)


def total(parts):
    value = parts[0].astype(jnp.float32)
    for part in parts[1:]:
        value = value + part.astype(jnp.float32)
    return value


def gather_plane(shard):
    row = jnp.stack([shard] + [send(shard, across(n)) for n in STEPS[1:]])
    own = [row] + [send(row, beside(n)) for n in STEPS[1:]]
    return own + [send(part, other_core) for part in own]


def scatter_plane(parts):
    kept = [None] * 4
    for n in (3, 1, 2, 0):
        kept[n] = total([parts[n], send(parts[4 + n], other_core)]).astype(jnp.bfloat16)
    row = [kept[0]] + [send(kept[n], beside(STEPS[n])) for n in (3, 1, 2)]
    row = total(row).astype(jnp.bfloat16)
    return [row[0]] + [send(row[n], across(STEPS[n])) for n in (3, 1, 2)]


def local(tokens, pattern, w_up, w_down, cotangent):
    dp, mp = lax.axis_index("dp"), lax.axis_index("mp")
    x, y, z, core = mp // 4, (dp // 8) * 2 + (mp // 2) % 2, dp % 8, mp % 2
    yh = dp // 8
    bf16, f32 = jnp.bfloat16, jnp.float32

    steps = jnp.array(STEPS, jnp.int32)
    def spots_of(c_at):
        first, second = steps[None, :], steps[:, None]
        x_at = (x - jnp.where(c_at == 0, first, second)) % 4
        y_at = (y - jnp.where(c_at == 0, second, first)) % 4
        return (x_at * 4 + (y_at % 2) * 2 + c_at) * 2 + y_at // 2

    spots = jnp.concatenate([spots_of(core).reshape(-1), spots_of(1 - core).reshape(-1)])
    spots = spots.astype(jnp.int32)
    own_rows = lax.dynamic_slice_in_dim(pattern, yh * 4, 4, 0)
    rows = jnp.where(yh == 0, own_rows, jnp.roll(own_rows, 8, axis=1))
    order = jnp.array([0, 1, 3, 2], jnp.int32)
    p_all = jnp.arange(64, dtype=jnp.int32)[:, None]
    c_to = (p_all // 4) % 2
    y_to = jnp.arange(2, dtype=jnp.int32)[None, :] * 2 + (p_all // 8) % 2
    x_step = order[(p_all // 16 - x) % 4] + 0 * y_to
    y_step = order[(y_to - y) % 4]
    first, second = jnp.where(c_to == 0, x_step, y_step), jnp.where(c_to == 0, y_step, x_step)
    outs_at = (((c_to ^ core) * 4 + second) * 4 + first).reshape(-1).astype(jnp.int32)

    both = jnp.stack([w_up[:, 0], w_down[:, 0]])
    other_b = send(lax.dynamic_slice_in_dim(both, (1 - yh) * 4, 4, 1), other_half)
    both = jnp.stack(lax.optimization_barrier((w_up[:, 0], w_down[:, 0])))
    piece_a = lax.dynamic_slice_in_dim(both, yh * 4, 4, 1)
    plane = gather_plane(jnp.stack([tokens, cotangent]))
    weights = lax.all_gather(
        jnp.stack([piece_a, other_b]), "dp", axis_index_groups=HALVES
    )

    gathered = jax.ShapeDtypeStruct((16, 2 * B, 4 * B), bf16)
    xs, gs = pl.pallas_call(
        place_kernel,
        out_shape=[gathered] * 2,
        in_specs=[SMEM] + [ANY] * 8,
        out_specs=[HBM] * 2,
        scratch_shapes=[
            pltpu.VMEM((16, 2 * B, 4 * B), bf16),
            pltpu.VMEM((16, 2 * B, 4 * B), bf16),
            pltpu.SemaphoreType.DMA((32,)),
            pltpu.SemaphoreType.DMA((32,)),
            pltpu.SemaphoreType.DMA((2,)),
        ],
        compiler_params=pltpu.CompilerParams(vmem_limit_bytes=56 * MIB),
        cost_estimate=pl.CostEstimate(flops=0, bytes_accessed=16 * MIB, transcendentals=0),
        name="place",
    )(spots, *plane)
    act, gh, grads = pl.pallas_call(
        first_kernel,
        out_shape=[jax.ShapeDtypeStruct((4, 2 * B, B), bf16)] * 2
        + [jax.ShapeDtypeStruct((8, 2, 2, 4, B, B), bf16)],
        in_specs=[HBM, HBM, HBM, HBM],
        out_specs=[VMEM, VMEM, HBM],
        scratch_shapes=[
            pltpu.VMEM((4, 8, 2, 2 * B, B), bf16),
            pltpu.VMEM((4, 8, 2, 2 * B, B), bf16),
            pltpu.VMEM((4, 8, 2, 2, B, B), bf16),
            pltpu.VMEM((4, 8, 2, 2, B, B), bf16),
            pltpu.SMEM((4, 16), jnp.int32),
            pltpu.SemaphoreType.DMA((4,)),
            pltpu.SemaphoreType.DMA((4,)),
            pltpu.SemaphoreType.DMA((4,)),
            pltpu.SemaphoreType.DMA((4, 2)),
            pltpu.SemaphoreType.DMA,
        ],
        compiler_params=pltpu.CompilerParams(vmem_limit_bytes=58 * MIB),
        cost_estimate=pl.CostEstimate(
            flops=2_000_000_000, bytes_accessed=16 * MIB, transcendentals=0
        ),
        name="first",
    )(rows, xs, gs, weights)

    summed = lax.psum_scatter(
        grads, "dp", scatter_dimension=0, axis_index_groups=HALVES, tiled=True
    )[0]

    parts = pl.pallas_call(
        second_kernel,
        out_shape=[jax.ShapeDtypeStruct((4, 2, B, 4 * B), bf16)] * 8,
        in_specs=[SMEM, SMEM, VMEM, VMEM, HBM],
        out_specs=[HBM] * 8,
        scratch_shapes=[
            pltpu.VMEM((4, 8, 2, 2, B, B), bf16),
            pltpu.VMEM((64, 2 * B, B), f32),
            pltpu.VMEM((64, 2 * B, B), f32),
            pltpu.VMEM((16, 2, 2, B, 4 * B), bf16),
            pltpu.SemaphoreType.DMA((4,)),
            pltpu.SemaphoreType.DMA,
        ],
        compiler_params=pltpu.CompilerParams(vmem_limit_bytes=58 * MIB),
        cost_estimate=pl.CostEstimate(
            flops=1_000_000_000, bytes_accessed=16 * MIB, transcendentals=0
        ),
        name="second",
    )(outs_at, rows, act, gh, weights)

    last = scatter_plane(parts)
    def assemble(own, other):
        halves = jnp.where(
            yh == 0, jnp.concatenate([own, other]), jnp.concatenate([other, own])
        )
        return halves.astype(f32)[:, None]

    other_down = send(summed[1, 1], other_half)
    other_up = send(jnp.swapaxes(summed[1, 0], 1, 2), other_half)
    own_up = jnp.swapaxes(lax.optimization_barrier(summed[0, 0]), 1, 2)
    last, other_down = lax.optimization_barrier((last, other_down))
    grad_down = assemble(summed[0, 1], other_down)
    grad_up = assemble(own_up, other_up)
    result = total(last).astype(bf16)
    mixed, grad_tokens = result[0], result[1]
    return mixed, grad_tokens, grad_up, grad_down


def solution(mesh):
    return jax.shard_map(
        local,
        mesh=mesh,
        in_specs=(
            P("dp", "mp"),
            P("mp", None),
            P("mp", "dp", None, None),
            P("mp", "dp", None, None),
            P("dp", "mp"),
        ),
        out_specs=(
            P("dp", "mp"),
            P("dp", "mp"),
            P("mp", "dp", None, None),
            P("mp", "dp", None, None),
        ),
        check_vma=False,
    )
```

```python
import jax
import jax.numpy as jnp
from jax import lax
from jax.experimental import pallas as pl
from jax.experimental.pallas import tpu as pltpu
from jax.sharding import PartitionSpec as P

AXES = ("dp", "mp")
B = 128
MIB = 1 << 20
GELU_C = 0.7978845608028654
GELU_A = 0.044715


def where_is(index):
    dp, mp = divmod(index, 16)
    return mp // 4, (dp // 8) * 2 + (mp // 2) % 2, dp % 8, mp % 2


def place_of(x, y, z, core):
    return ((y // 2) * 8 + z) * 16 + x * 4 + (y % 2) * 2 + core


def send(value, step):
    return lax.ppermute(
        value, AXES, [(source, place_of(*step(*where_is(source)))) for source in range(256)]
    )


def across(steps):
    return lambda x, y, z, c: ((x + steps * (1 - c)) % 4, (y + steps * c) % 4, z, c)


def beside(steps):
    return lambda x, y, z, c: ((x + steps * c) % 4, (y + steps * (1 - c)) % 4, z, c)


def other_core(x, y, z, c):
    return x, y, z, 1 - c


def other_half(x, y, z, c):
    return x, (y + 2) % 4, z, c


def gelu_parts(h):
    t = jnp.tanh(GELU_C * (h + GELU_A * (h * h * h)))
    half = 0.5 * (1.0 + t)
    slope = half + 0.5 * h * (1.0 - t * t) * (GELU_C * (1.0 + 3.0 * GELU_A * (h * h)))
    return h * half, slope


NT = (((1,), (1,)), ((), ()))


def dot(a, b, dims=(((1,), (0,)), ((), ()))):
    return lax.dot_general(a, b, dims, preferred_element_type=jnp.float32)


def place_kernel(spots, *refs):
    parts, x_out, g_out = refs[:8], refs[8], refs[9]
    xs, gs, sem_x, sem_g, sem_out = refs[10:]
    copies = ([], [])
    for m, (scratch, sems) in enumerate(((xs, sem_x), (gs, sem_g))):
        for n in range(8):
            for r in range(4):
                spot = spots[n * 4 + r]
                half = pl.ds(pl.multiple_of((spot % 2) * B, B), B)
                copies[m].append(
                    pltpu.make_async_copy(
                        parts[n].at[r, m], scratch.at[spot // 2, half], sems.at[n * 4 + r]
                    )
                )
    for copy in copies[0] + copies[1]:
        copy.start()
    stores = (
        pltpu.make_async_copy(xs, x_out, sem_out.at[0]),
        pltpu.make_async_copy(gs, g_out, sem_out.at[1]),
    )
    for m in range(2):
        for copy in copies[m]:
            copy.wait()
        stores[m].start()
    for store in stores:
        store.wait()


def first_kernel(rows_in, x_in, g_in, w_in, act_out, gh_out, grads_out, *scratch):
    xs, gs, ws, grads, rows, sem_x, sem_g, sem_in, sem_out, sem_rows = scratch

    def store(j, half):
        slots = pl.ds(4 * half, 4)
        return pltpu.make_async_copy(
            grads.at[j, slots], grads_out.at[slots, :, :, j], sem_out.at[j, half]
        )

    def load_w(j):
        return pltpu.make_async_copy(w_in.at[:, :, :, j], ws.at[j], sem_in.at[j])

    def load(j):
        for source, target, sems in ((x_in, xs, sem_x), (g_in, gs, sem_g)):
            for s in range(8):
                for half in range(2):
                    p = rows[j, half * 8 + s]
                    lanes = pl.ds(pl.multiple_of((p % 4) * B, B), B)
                    pltpu.make_async_copy(
                        source.at[p // 4, :, lanes], target.at[j, s, half], sems.at[j]
                    ).start()

    def pick(scratch, j, s):
        return jnp.concatenate([scratch[j, s, 0], scratch[j, s, 1]], axis=1)

    def two_columns(i, carry):
        @pl.when(i < 1)
        def _():
            for j in (2, 3):
                load_w(j).start()
                load(j)

        pair = (2 * i, 2 * i + 1)
        for j in pair:
            for target, sems in ((xs, sem_x), (gs, sem_g)):
                pltpu.make_async_copy(target.at[j], target.at[j], sems.at[j]).wait()
            load_w(j).wait()
        hidden = [jnp.zeros((2 * B, B), jnp.float32)] * 2
        grad_act = [jnp.zeros((2 * B, B), jnp.float32)] * 2
        for s in range(8):
            for n, j in enumerate(pair):
                up = jnp.concatenate([ws[j, s, 0, 0], ws[j, s, 1, 0]], axis=0)
                hidden[n] += dot(pick(xs, j, s), up)
                down = jnp.concatenate([ws[j, s, 0, 1], ws[j, s, 1, 1]], axis=1)
                grad_act[n] += dot(pick(gs, j, s), down, NT)
        turned = []
        for n, j in enumerate(pair):
            value, slope = gelu_parts(hidden[n])
            grad_hidden = slope * grad_act[n]
            act_out[j] = value.astype(jnp.bfloat16)
            gh_out[j] = grad_hidden.astype(jnp.bfloat16)
            turned.append((value.T.astype(jnp.bfloat16), grad_hidden.T.astype(jnp.bfloat16)))
        for n, j in enumerate(pair):
            act_t, gh_t = turned[n]
            for s in range(8):
                up = dot(gh_t, pick(xs, j, s)).astype(jnp.bfloat16)
                grads[j, s, 0, 0] = up[:, :B]
                grads[j, s, 1, 0] = up[:, B:]
                down = dot(act_t, pick(gs, j, s)).astype(jnp.bfloat16)
                grads[j, s, 0, 1] = down[:, :B]
                grads[j, s, 1, 1] = down[:, B:]
                if s % 4 == 3:
                    store(j, s // 4).start()
        return carry

    fetch = pltpu.make_async_copy(rows_in, rows, sem_rows)
    fetch.start()
    for j in (0, 1):
        load_w(j).start()
    fetch.wait()
    for j in (0, 1):
        load(j)
    lax.fori_loop(0, 2, two_columns, 0)
    for j in range(4):
        for half in range(2):
            store(j, half).wait()


def second_kernel(outs_at, rows, act_ref, gh_ref, *refs):
    w_in, parts = refs[0], refs[1:9]
    ws, out_acc, in_acc, stage, sem_w, sem_out = refs[9:]

    def load(j):
        return pltpu.make_async_copy(w_in.at[:, :, :, j], ws.at[j], sem_w.at[j])

    for j in range(4):
        load(j).start()

    def clear(p, carry):
        out_acc[p] = jnp.zeros((2 * B, B), jnp.float32)
        in_acc[p] = jnp.zeros((2 * B, B), jnp.float32)
        return carry

    lax.fori_loop(0, 64, clear, 0)

    def two_columns(i, carry):
        pair = (2 * i, 2 * i + 1)
        for j in pair:
            load(j).wait()
        for s in range(8):
            terms = []
            for j in pair:
                down = jnp.concatenate([ws[j, s, 0, 1], ws[j, s, 1, 1]], axis=1)
                up = jnp.concatenate([ws[j, s, 0, 0], ws[j, s, 1, 0]], axis=0)
                terms.append((dot(act_ref[j], down), dot(gh_ref[j], up, NT)))
            for j, (out_term, in_term) in zip(pair, terms):
                for half in range(2):
                    p = rows[j, half * 8 + s]
                    out_acc[p] += out_term[:, half * B : (half + 1) * B]
                    in_acc[p] += in_term[:, half * B : (half + 1) * B]
        return carry

    lax.fori_loop(0, 2, two_columns, 0)

    def finish(m, carry):
        for half in range(2):
            rows_of = pl.ds(half * B, B)
            for n in range(4):
                lanes = pl.ds(n * B, B)
                stage[m, half, 0, :, lanes] = out_acc[m * 4 + n, rows_of].astype(jnp.bfloat16)
                stage[m, half, 1, :, lanes] = in_acc[m * 4 + n, rows_of].astype(jnp.bfloat16)
            at = outs_at[m * 8 + half]
            for n, part in enumerate(parts):

                @pl.when(at // 4 == n)
                def _(part=part):
                    pltpu.make_async_copy(stage.at[m, half], part.at[at % 4], sem_out).start()

        return carry

    lax.fori_loop(0, 16, finish, 0)
    pltpu.make_async_copy(stage, stage, sem_out).wait()


SMEM = pl.BlockSpec(memory_space=pltpu.SMEM)
VMEM = pl.BlockSpec(memory_space=pltpu.VMEM)
ANY = pl.BlockSpec(memory_space=pl.ANY)
HBM = pl.BlockSpec(memory_space=pltpu.HBM)
HALVES = [list(range(8)), list(range(8, 16))]
STEPS = (0, 1, 3, 2)


def total(parts):
    value = parts[0].astype(jnp.float32)
    for part in parts[1:]:
        value = value + part.astype(jnp.float32)
    return value


def gather_plane(shard):
    row = jnp.stack([shard] + [send(shard, across(n)) for n in STEPS[1:]])
    own = [row] + [send(row, beside(n)) for n in STEPS[1:]]
    return own + [send(part, other_core) for part in own]


def scatter_plane(parts):
    kept = [None] * 4
    for n in (3, 1, 2, 0):
        kept[n] = total([parts[n], send(parts[4 + n], other_core)]).astype(jnp.bfloat16)
    row = [kept[0]] + [send(kept[n], beside(STEPS[n])) for n in (3, 1, 2)]
    row = total(row).astype(jnp.bfloat16)
    return [row[0]] + [send(row[n], across(STEPS[n])) for n in (3, 1, 2)]


def local(tokens, pattern, w_up, w_down, cotangent):
    dp, mp = lax.axis_index("dp"), lax.axis_index("mp")
    x, y, z, core = mp // 4, (dp // 8) * 2 + (mp // 2) % 2, dp % 8, mp % 2
    yh = dp // 8
    bf16, f32 = jnp.bfloat16, jnp.float32

    steps = jnp.array(STEPS, jnp.int32)
    def spots_of(c_at):
        first, second = steps[None, :], steps[:, None]
        x_at = (x - jnp.where(c_at == 0, first, second)) % 4
        y_at = (y - jnp.where(c_at == 0, second, first)) % 4
        return (x_at * 4 + (y_at % 2) * 2 + c_at) * 2 + y_at // 2

    spots = jnp.concatenate([spots_of(core).reshape(-1), spots_of(1 - core).reshape(-1)])
    spots = spots.astype(jnp.int32)
    own_rows = lax.dynamic_slice_in_dim(pattern, yh * 4, 4, 0)
    rows = jnp.where(yh == 0, own_rows, jnp.roll(own_rows, 8, axis=1))
    order = jnp.array([0, 1, 3, 2], jnp.int32)
    p_all = jnp.arange(64, dtype=jnp.int32)[:, None]
    c_to = (p_all // 4) % 2
    y_to = jnp.arange(2, dtype=jnp.int32)[None, :] * 2 + (p_all // 8) % 2
    x_step = order[(p_all // 16 - x) % 4] + 0 * y_to
    y_step = order[(y_to - y) % 4]
    first, second = jnp.where(c_to == 0, x_step, y_step), jnp.where(c_to == 0, y_step, x_step)
    outs_at = (((c_to ^ core) * 4 + second) * 4 + first).reshape(-1).astype(jnp.int32)

    both = jnp.stack([w_up[:, 0], w_down[:, 0]])
    other_b = send(lax.dynamic_slice_in_dim(both, (1 - yh) * 4, 4, 1), other_half)
    both = jnp.stack(lax.optimization_barrier((w_up[:, 0], w_down[:, 0])))
    piece_a = lax.dynamic_slice_in_dim(both, yh * 4, 4, 1)
    plane = gather_plane(jnp.stack([tokens, cotangent]))
    weights = lax.all_gather(
        jnp.stack([piece_a, other_b]), "dp", axis_index_groups=HALVES
    )

    gathered = jax.ShapeDtypeStruct((16, 2 * B, 4 * B), bf16)
    xs, gs = pl.pallas_call(
        place_kernel,
        out_shape=[gathered] * 2,
        in_specs=[SMEM] + [ANY] * 8,
        out_specs=[HBM] * 2,
        scratch_shapes=[
            pltpu.VMEM((16, 2 * B, 4 * B), bf16),
            pltpu.VMEM((16, 2 * B, 4 * B), bf16),
            pltpu.SemaphoreType.DMA((32,)),
            pltpu.SemaphoreType.DMA((32,)),
            pltpu.SemaphoreType.DMA((2,)),
        ],
        compiler_params=pltpu.CompilerParams(vmem_limit_bytes=56 * MIB),
        cost_estimate=pl.CostEstimate(flops=0, bytes_accessed=16 * MIB, transcendentals=0),
        name="place",
    )(spots, *plane)
    act, gh, grads = pl.pallas_call(
        first_kernel,
        out_shape=[jax.ShapeDtypeStruct((4, 2 * B, B), bf16)] * 2
        + [jax.ShapeDtypeStruct((8, 2, 2, 4, B, B), bf16)],
        in_specs=[HBM, HBM, HBM, HBM],
        out_specs=[VMEM, VMEM, HBM],
        scratch_shapes=[
            pltpu.VMEM((4, 8, 2, 2 * B, B), bf16),
            pltpu.VMEM((4, 8, 2, 2 * B, B), bf16),
            pltpu.VMEM((4, 8, 2, 2, B, B), bf16),
            pltpu.VMEM((4, 8, 2, 2, B, B), bf16),
            pltpu.SMEM((4, 16), jnp.int32),
            pltpu.SemaphoreType.DMA((4,)),
            pltpu.SemaphoreType.DMA((4,)),
            pltpu.SemaphoreType.DMA((4,)),
            pltpu.SemaphoreType.DMA((4, 2)),
            pltpu.SemaphoreType.DMA,
        ],
        compiler_params=pltpu.CompilerParams(vmem_limit_bytes=58 * MIB),
        cost_estimate=pl.CostEstimate(
            flops=2_000_000_000, bytes_accessed=16 * MIB, transcendentals=0
        ),
        name="first",
    )(rows, xs, gs, weights)

    summed = lax.psum_scatter(
        grads, "dp", scatter_dimension=0, axis_index_groups=HALVES, tiled=True
    )[0]

    parts = pl.pallas_call(
        second_kernel,
        out_shape=[jax.ShapeDtypeStruct((4, 2, B, 4 * B), bf16)] * 8,
        in_specs=[SMEM, SMEM, VMEM, VMEM, HBM],
        out_specs=[HBM] * 8,
        scratch_shapes=[
            pltpu.VMEM((4, 8, 2, 2, B, B), bf16),
            pltpu.VMEM((64, 2 * B, B), f32),
            pltpu.VMEM((64, 2 * B, B), f32),
            pltpu.VMEM((16, 2, 2, B, 4 * B), bf16),
            pltpu.SemaphoreType.DMA((4,)),
            pltpu.SemaphoreType.DMA,
        ],
        compiler_params=pltpu.CompilerParams(vmem_limit_bytes=58 * MIB),
        cost_estimate=pl.CostEstimate(
            flops=1_000_000_000, bytes_accessed=16 * MIB, transcendentals=0
        ),
        name="second",
    )(outs_at, rows, act, gh, weights)

    last = scatter_plane(parts)
    def assemble(own, other):
        halves = jnp.where(
            yh == 0, jnp.concatenate([own, other]), jnp.concatenate([other, own])
        )
        return halves.astype(f32)[:, None]

    other_up = send(jnp.swapaxes(summed[1, 0], 1, 2), other_half)
    other_down = send(summed[1, 1], other_half)
    own_up = jnp.swapaxes(lax.optimization_barrier(summed[0, 0]), 1, 2)
    last, other_up = lax.optimization_barrier((last, other_up))
    grad_down = assemble(summed[0, 1], other_down)
    grad_up = assemble(own_up, other_up)
    result = total(last).astype(bf16)
    mixed, grad_tokens = result[0], result[1]
    return mixed, grad_tokens, grad_up, grad_down


def solution(mesh):
    return jax.shard_map(
        local,
        mesh=mesh,
        in_specs=(
            P("dp", "mp"),
            P("mp", None),
            P("mp", "dp", None, None),
            P("mp", "dp", None, None),
            P("dp", "mp"),
        ),
        out_specs=(
            P("dp", "mp"),
            P("dp", "mp"),
            P("mp", "dp", None, None),
            P("mp", "dp", None, None),
        ),
        check_vma=False,
    )
```
